32 devices in a mesh: bank: 4 (over y, x), seg: 8 (over z, core).
Axes of the slice: x: 2, y: 2, z: 4, core: 2. Of those that a mesh axis runs over, the one named last changes fastest.
Arguments:
- strain: bfloat16 [64, 2, 2, 65536], P(('bank', 'seg')), may hold values from -6 to 6
- templates: bfloat16 [4, 2, 65536], P('bank', None, 'seg'), may hold values from -0.0234375 to 0.0234375
- bin_edges: int32 [4, 15], replicated, may hold values from 1 to 255, as said below
- live_flags: int32 [64], P(('bank', 'seg')), may hold values from 0 to 1, as said below
Outputs:
- peak_snr: float32 [4, 64], P(None, ('bank', 'seg'))
- coarse_snr: float32 [4, 64, 256], P(None, ('bank', 'seg'))
- chi_series: float32 [4, 64, 256], P(None, ('bank', 'seg'))
The draws below stay inside these ranges and needn't reach their ends.
Inputs may be any that keep to these rules, and one draw needn't show every extreme that they name: `bin_edges`: each row rises strictly. `live_flags`: on each device the live slots (1) come first; two devices whose indices along seg differ only in the lowest bit hold exactly 2 live slots together; some device holds 2 live slots.
All inputs are finite; a program needn't handle non-finite values.
Results may differ from the reference program's by a relative error of at most 0.0025.
Values may be sent and summed in bfloat16 or wider, within the bound.
No kernel may reach another device: no remote copies, remote signals or barrier semaphores. Data moves between devices by JAX's collectives and lax.ppermute only.
A program may use at most 64 MiB of HBM per device.

```python
import math
import jax
import jax.numpy as jnp
from jax import lax

FREQ = 65536
FA = 256
FB = 256
BINS = 16
DET = 2
SLOT_DEV = 2
TEMPLATES = 4
SLOTS = 64


def draw_bin_edges(key, part):
    key = jax.random.fold_in(key, 11)
    keys = jax.random.split(key, TEMPLATES)

    def one(single):
        picked = jax.random.permutation(single, FB - 1)[:BINS - 1] + 1
        return jnp.sort(picked)
    return jax.vmap(one)(keys).astype(jnp.int32)


def draw_live_flags(key, part):
    key = jax.random.fold_in(key, 23)
    first_key, full_key = jax.random.split(key)
    pairs = SLOTS // (2 * SLOT_DEV)
    first = jax.random.randint(first_key, (pairs,), 0, SLOT_DEV + 1)
    chosen = jax.random.randint(full_key, (), 0, pairs)
    first = jnp.where(jnp.arange(pairs) == chosen, SLOT_DEV, first)
    counts = jnp.stack([first, SLOT_DEV - first], axis=1).reshape(-1)
    slot_index = jnp.arange(SLOT_DEV)
    return (slot_index[None, :] < counts[:, None]).astype(jnp.int32).reshape(SLOTS)


def block_levels(rng, extent, pieces, smallest, top_value):
    gain, own = 1.0, jax.random.fold_in(rng, 6)
    for position, blocks in pieces:
        heights = jnp.exp(jax.random.uniform(jax.random.fold_in(own, position), (blocks,), jnp.float32, smallest / len(pieces), top_value / len(pieces)))
        gain = gain * jnp.repeat(heights, extent[position] // blocks).reshape([-1 if axis == position else 1 for axis in range(len(extent))])
    return gain


def scatter_about(key, extent, deviation, limit, pieces=(), kind=jnp.bfloat16):
    drawn = jax.random.normal(key, extent, jnp.float32) * deviation
    if len(pieces) > 0:
        drawn = block_levels(key, extent, pieces, -0.22, 0.18) * drawn
    return jnp.clip(drawn, min=-limit, max=limit).astype(kind)


def setup_inputs(seed: int = 0) -> dict:
    key_of = jax.random.split(jax.random.key(seed), 5)
    return {
        "strain": scatter_about(key_of[0], (SLOTS, DET, 2, FREQ), 1.0, 6.0, ((0, 32),)),
        "templates": scatter_about(key_of[1], (TEMPLATES, 2, FREQ), FREQ ** -0.5, 0.0234375, ((0, 4), (2, 8))),
        "bin_edges": draw_bin_edges(jax.random.fold_in(key_of[4], 71), 0),
        "live_flags": draw_live_flags(jax.random.fold_in(key_of[4], 71), 0),
    }


def complex_table(rows, cols, length, dtype):
    left = jnp.arange(rows, dtype=jnp.int32)[:, None]
    right = jnp.arange(cols, dtype=jnp.int32)[None, :]
    angle = (left * right % length).astype(jnp.float32) * (2.0 * math.pi / length)
    cosine = jnp.cos(angle).astype(dtype)
    sine = jnp.sin(angle).astype(dtype)
    upper = jnp.stack([cosine, sine], axis=1)
    lower = jnp.stack([-sine, cosine], axis=1)
    return jnp.stack([upper, lower], axis=0)

def twiddles():
    left = jnp.arange(FA, dtype=jnp.int32)[:, None]
    right = jnp.arange(FB, dtype=jnp.int32)[None, :]
    angle = (left * right % FREQ).astype(jnp.float32) * (2.0 * math.pi / FREQ)
    return (jnp.cos(angle), jnp.sin(angle))

def bin_table(edges):
    blocks = jnp.arange(FB, dtype=jnp.int32)
    labels = lax.optimization_barrier(jnp.sum((edges[:, :, None] <= blocks[None, None, :]).astype(jnp.int32), axis=1))
    return (labels[:, None, :] == jnp.arange(BINS, dtype=jnp.int32)[None, :, None]).astype(jnp.bfloat16)

def accumulate(carry, spectra, piece, start, onehot):
    prodbuf, binsum, hsq = carry
    width = piece.shape[-1]
    rows = width // FA
    row0 = start // FA
    window = lax.dynamic_slice_in_dim(spectra, start, width, 3)
    sre = window[:, :, 0].astype(jnp.float32)[None]
    sim = window[:, :, 1].astype(jnp.float32)[None]
    hre = piece[:, 0].astype(jnp.float32)
    him = piece[:, 1].astype(jnp.float32)
    hre_b = hre[:, None, None, :]
    him_b = him[:, None, None, :]
    real_part = sre * hre_b + sim * him_b
    imag_part = sim * hre_b - sre * him_b
    product = jnp.stack([real_part, imag_part], axis=3).astype(jnp.bfloat16)
    product = product.reshape(product.shape[:4] + (rows, FA))
    prodbuf = lax.dynamic_update_slice_in_dim(prodbuf, product, row0, 4)
    ohrows = lax.dynamic_slice_in_dim(onehot, row0, rows, 2)
    binsum = binsum + jnp.einsum('tbf,tsdcfa->tsdcba', ohrows, product, preferred_element_type=jnp.float32)
    rowpower = lax.optimization_barrier(jnp.sum((hre * hre + him * him).reshape(hre.shape[0], rows, FA), axis=-1))
    current = lax.dynamic_slice_in_dim(hsq, row0, rows, 1)
    hsq = lax.dynamic_update_slice_in_dim(hsq, current + rowpower, row0, 1)
    return (prodbuf, binsum, hsq)

def finish(carry, onehot, wbig, wa_table, wc_table, tw_cos, tw_sin):
    prodbuf, binsum, hsq = carry
    first = jnp.einsum('tsdcfa,cfox->tsdaox', prodbuf, wbig, preferred_element_type=jnp.float32)
    are = first[..., 0, :]
    aim = first[..., 1, :]
    bre = are * tw_cos - aim * tw_sin
    bim = are * tw_sin + aim * tw_cos
    turned = jnp.stack([bre, bim], axis=-2).astype(jnp.bfloat16)
    series = jnp.einsum('tsdacx,caou->tsdoux', turned, wa_table, preferred_element_type=jnp.float32)
    hpower = jnp.einsum('tbf,tf->tb', onehot.astype(jnp.float32), hsq, precision=lax.Precision.HIGHEST)
    sigma = lax.optimization_barrier(jnp.sum(hpower, axis=-1))
    power = lax.optimization_barrier(jnp.sum(series * series, axis=(2, 3)))
    peak = jnp.sqrt(lax.optimization_barrier(jnp.max(power, axis=(2, 3))) / sigma[:, None])
    part = jnp.einsum('tsdcba,caok->tsdobk', binsum, wc_table, precision=lax.Precision.HIGHEST)
    whole = lax.optimization_barrier(jnp.sum(part, axis=4))
    share = hpower / sigma[:, None]
    diff = part - share[:, None, None, None, :, None] * whole[:, :, :, :, None, :]
    chi = lax.optimization_barrier(jnp.sum(diff * diff, axis=(2, 3, 4))) / sigma[:, None, None] / (4.0 * (BINS - 1))
    coarse = lax.optimization_barrier(jnp.sum(whole * whole, axis=(2, 3))) / sigma[:, None, None]
    return (peak, coarse, chi)

def reference(strain, templates, bin_edges, live_flags):
    wbig = complex_table(FB, FB, FB, jnp.bfloat16)
    wa_table = complex_table(FA, FA, FA, jnp.bfloat16)
    wc_table = complex_table(FA, FB, FB, jnp.float32)
    tw_cos, tw_sin = twiddles()
    onehot = bin_table(bin_edges)
    count = TEMPLATES

    def one(index):
        spectra = lax.dynamic_slice_in_dim(strain, index, 1, 0)
        init = (jnp.zeros((count, 1, DET, 2, FB, FA), jnp.bfloat16), jnp.zeros((count, 1, DET, 2, BINS, FA), jnp.float32), jnp.zeros((count, FB), jnp.float32))
        carry = accumulate(init, spectra, templates, 0, onehot)
        return finish(carry, onehot, wbig, wa_table, wc_table, tw_cos, tw_sin)
    live = jnp.nonzero(live_flags, size=SLOTS // 2)[0].astype(jnp.int32)
    peaks, coarses, chis = lax.map(one, live)
    peak_snr = jnp.zeros((TEMPLATES, SLOTS), jnp.float32).at[:, live].set(jnp.transpose(peaks[:, :, 0]))
    coarse_snr = jnp.zeros((TEMPLATES, SLOTS, FB), jnp.float32).at[:, live].set(jnp.transpose(coarses[:, :, 0], (1, 0, 2)))
    chi_series = jnp.zeros((TEMPLATES, SLOTS, FB), jnp.float32).at[:, live].set(jnp.transpose(chis[:, :, 0], (1, 0, 2)))
    return (peak_snr, coarse_snr, chi_series)
```

```python
import functools
import math

import jax
import jax.numpy as jnp
import numpy as np
from jax import lax
from jax.experimental import pallas as pl
from jax.experimental.pallas import tpu as pltpu
from jax.sharding import PartitionSpec as P

FA = 256
FB = 256
HALF = 128
BINS = 16
BF16 = jnp.bfloat16
F32 = jnp.float32


def waves(rows, cols, length):
    turns = np.outer(rows, cols) % length
    angle = turns * (2.0 * math.pi / length)
    return np.cos(angle), np.sin(angle)


def tables():
    bf = np.dtype(BF16)
    every = np.arange(FA)
    cosine, sine = waves(every, every, FA)
    first = np.block([[cosine, -sine], [sine, cosine]]).astype(bf)
    half = np.arange(HALF)
    even_c, even_s = waves(half, 2 * half, FA)
    odd_c, odd_s = waves(half, 2 * half + 1, FA)
    second = np.stack(
        [
            np.block([[even_c, even_s], [-even_s, even_c]]),
            np.block([[odd_c, odd_s], [-odd_s, odd_c]]),
        ]
    ).astype(bf)
    coarse = np.block([[cosine, sine], [-sine, cosine]]).astype(np.float32)
    upper = coarse.astype(bf)
    lower = (coarse - upper.astype(np.float32)).astype(bf)
    turn = np.stack(waves(every, every, FA * FB)).astype(np.float32)
    return first, second, np.stack([upper, lower]), turn


def dot(left, right):
    return jnp.dot(left, right, preferred_element_type=F32)


def split(value):
    upper = value.astype(BF16)
    return upper, (value - upper.astype(F32)).astype(BF16)


def flip_orders(nbank, nseg):
    seg = [(0, 1 << k) for k in range(1, nseg.bit_length() - 1)]
    bank = [(1 << k, 0) for k in range(nbank.bit_length() - 1)]
    return (seg[::-1] + bank, seg + bank[::-1]), len(seg)


def reach(order, place):
    bank = seg = 0
    for k, (b, s) in enumerate(order):
        if place >> k & 1:
            bank, seg = bank ^ b, seg ^ s
    return bank, seg


def filter_body(
    nbank, nseg, held, tiles, live_ref, edges_ref, strain_ref, mine0, mine1, theirs0, theirs1,
    first_ref, second_ref, coarse_ref, turn_ref, peak_ref, snr_ref, chi_ref,
    left, spectrum, product, turned, sums, hpow,
):
    orders, seg_steps = flip_orders(nbank, nseg)
    my_bank = lax.axis_index("bank")
    my_seg = lax.axis_index("seg")
    core = my_seg & 1
    rows = FB // nseg
    total = nbank * tiles
    low = 1 << seg_steps
    places = 1 << len(orders[0])
    swapped = {reach(orders[1], p): p for p in range(places)}

    left[0 : 2 * FB] = first_ref[...]
    peak_ref[...] = jnp.zeros(peak_ref.shape, F32)
    snr_ref[...] = jnp.zeros(snr_ref.shape, F32)
    chi_ref[...] = jnp.zeros(chi_ref.shape, F32)
    blocks = lax.broadcasted_iota(jnp.int32, (BINS, FB), 1)
    bins = lax.broadcasted_iota(jnp.int32, (BINS, FB), 0)

    def piece(refs, place, k):
        ref, at = (refs[0], place) if place < places // 2 else (refs[1], place - places // 2)
        return ref[at * tiles + k]

    for q in range(nbank):
        bank0 = reach(orders[0], q * low)[0]
        bank1 = reach(orders[1], q * low)[0]
        bank = my_bank ^ jnp.where(core == 0, bank0, bank1)
        partner_q = swapped[(bank0, 0)] // low
        for k in range(tiles):
            t = bank * tiles + k
            for z in range(low):
                seg0, seg1 = reach(orders[0], z)[1], reach(orders[1], z)[1]
                own = my_seg ^ jnp.where(core == 0, seg0, seg1)
                other = my_seg ^ 1 ^ jnp.where(core == 0, seg1, seg0)
                for refs, place, seg in (
                    ((mine0, mine1), q * low + z, own),
                    ((theirs0, theirs1), partner_q * low + z, other),
                ):
                    data = piece(refs, place, k).astype(F32)
                    start = pl.multiple_of(seg * rows, rows)
                    spectrum[:, pl.ds(start, rows), :] = data

            label = jnp.zeros((BINS, FB), jnp.int32)
            for j in range(BINS - 1):
                label = label + (edges_ref[t, j] <= blocks).astype(jnp.int32)
            onehot = (label == bins).astype(F32).astype(BF16)
            nothing = jnp.zeros((BINS, FB), BF16)
            left[2 * FB : 2 * FB + BINS, 0:FB] = onehot
            left[2 * FB : 2 * FB + BINS, FB:] = nothing
            left[2 * FB + BINS :, 0:FB] = nothing
            left[2 * FB + BINS :, FB:] = onehot

            energy = spectrum[0] * spectrum[0] + spectrum[1] * spectrum[1]
            energy = energy[:, :HALF] + energy[:, HALF:]
            upper, lower = split(energy)
            power = dot(onehot, upper) + dot(onehot, lower)
            hpower = jnp.sum(power, axis=1, keepdims=True)
            sigma = jnp.sum(hpower, axis=0, keepdims=True)
            share = hpower / sigma

            for s in range(held):

                @pl.when(live_ref[s] != 0)
                def _():
                    hre, him = spectrum[0], spectrum[1]
                    for d in range(2):
                        sre = strain_ref[s, d, 0].astype(F32)
                        sim = strain_ref[s, d, 1].astype(F32)
                        cols = slice(d * FA, (d + 1) * FA)
                        product[0:FB, cols] = (sre * hre + sim * him).astype(BF16)
                        product[FB:, cols] = (sim * hre - sre * him).astype(BF16)
                    for d in range(2):
                        cols = slice(d * FA, (d + 1) * FA)
                        one = dot(left[...], product[:, cols])
                        are, aim = one[0:FB], one[FB : 2 * FB]
                        bre = are * turn_ref[0] - aim * turn_ref[1]
                        bim = are * turn_ref[1] + aim * turn_ref[0]
                        lines = slice(d * FB, (d + 1) * FB)
                        turned[0, lines, 0:HALF] = (bre[:, :HALF] + bre[:, HALF:]).astype(BF16)
                        turned[0, lines, HALF:] = (bim[:, :HALF] + bim[:, HALF:]).astype(BF16)
                        turned[1, lines, 0:HALF] = (bre[:, :HALF] - bre[:, HALF:]).astype(BF16)
                        turned[1, lines, HALF:] = (bim[:, :HALF] - bim[:, HALF:]).astype(BF16)
                        here = slice(d * BINS, (d + 1) * BINS)
                        sums[here, 0:FA] = one[2 * FB : 2 * FB + BINS]
                        sums[here, FA:] = one[2 * FB + BINS :]
                    best = jnp.zeros((FB, HALF), F32)
                    for parity in range(2):
                        series = dot(turned[parity], second_ref[parity])
                        series = series * series
                        series = series[:FB] + series[FB:]
                        best = jnp.maximum(best, series[:, :HALF] + series[:, HALF:])
                    upper, lower = split(sums[...])
                    part = (
                        dot(upper, coarse_ref[0])
                        + dot(lower, coarse_ref[0])
                        + dot(upper, coarse_ref[1])
                    )
                    snr = jnp.zeros((1, FB), F32)
                    chi = jnp.zeros((1, FB), F32)
                    for d in range(2):
                        own = part[d * BINS : (d + 1) * BINS]
                        whole = jnp.sum(own, axis=0, keepdims=True)
                        diff = own - share * whole
                        diff = jnp.sum(diff * diff, axis=0, keepdims=True)
                        whole = whole * whole
                        snr = snr + whole[:, :FB] + whole[:, FB:]
                        chi = chi + diff[:, :FB] + diff[:, FB:]
                    snr_ref[t, s : s + 1] = snr / sigma
                    chi_ref[t, s : s + 1] = chi / sigma / (4.0 * (BINS - 1))
                    peak = jnp.max(jnp.max(best, axis=0, keepdims=True), axis=1, keepdims=True)
                    peak = jnp.sqrt(peak / sigma)
                    at = (lax.broadcasted_iota(jnp.int32, peak_ref.shape, 0) == t) & (
                        lax.broadcasted_iota(jnp.int32, peak_ref.shape, 1) == s
                    )
                    peak_ref[...] = jnp.where(at, peak, peak_ref[...])


def on_device(nbank, nseg, strain, templates, bin_edges, live_flags):
    held = strain.shape[0]
    tiles = templates.shape[0]
    total = tiles * nbank
    rows = FB // nseg
    first, second, coarse, turn = (jnp.asarray(x) for x in tables())
    orders, _ = flip_orders(nbank, nseg)

    def swap(block, step):
        route = []
        for b in range(nbank):
            for s in range(nseg):
                flip_bank, flip_seg = (0, 1) if step is None else orders[s & 1][step]
                route.append((b * nseg + s, (b ^ flip_bank) * nseg + (s ^ flip_seg)))
        return lax.ppermute(block, ("bank", "seg"), route)

    block = templates.reshape(tiles, 2, rows, FA)
    steps = len(orders[0])
    for step in range(steps - 1):
        block = jnp.concatenate([block, swap(block, step)], axis=0)
    late = swap(block, steps - 1)
    other = swap(block, None)
    other_late = swap(late, None)
    whole = strain.reshape(held, 2, 2, FB, FA)

    body = functools.partial(filter_body, nbank, nseg, held, tiles)
    smem = pl.BlockSpec(memory_space=pltpu.SMEM)
    vmem = pl.BlockSpec(memory_space=pltpu.VMEM)
    return pl.pallas_call(
        body,
        in_specs=[smem, smem] + [vmem] * 9,
        out_specs=[vmem] * 3,
        out_shape=[
            jax.ShapeDtypeStruct((total, held), F32),
            jax.ShapeDtypeStruct((total, held, FB), F32),
            jax.ShapeDtypeStruct((total, held, FB), F32),
        ],
        scratch_shapes=[
            pltpu.VMEM((2 * FB + 2 * BINS, 2 * FB), BF16),
            pltpu.VMEM((2, FB, FA), F32),
            pltpu.VMEM((2 * FB, 2 * FA), BF16),
            pltpu.VMEM((2, 2 * FB, FA), BF16),
            pltpu.VMEM((2 * BINS, 2 * FA), F32),
            pltpu.VMEM((BINS, HALF), F32),
        ],
        compiler_params=pltpu.CompilerParams(vmem_limit_bytes=40 << 20),
    )(live_flags, bin_edges, whole, block, late, other, other_late, first, second, coarse, turn)


def solution(mesh):
    in_specs = (
        P(("bank", "seg"), None, None, None),
        P("bank", None, "seg"),
        P(),
        P(("bank", "seg")),
    )
    out_specs = (
        P(None, ("bank", "seg")),
        P(None, ("bank", "seg"), None),
        P(None, ("bank", "seg"), None),
    )
    body = functools.partial(on_device, mesh.shape["bank"], mesh.shape["seg"])
    return jax.shard_map(body, mesh=mesh, in_specs=in_specs, out_specs=out_specs, check_vma=False)
```

```python
import functools
import math

import jax
import jax.numpy as jnp
import numpy as np
from jax import lax
from jax.experimental import pallas as pl
from jax.experimental.pallas import tpu as pltpu
from jax.sharding import PartitionSpec as P

FA = 256
FB = 256
HALF = 128
BINS = 16
STEP = 16
BF16 = jnp.bfloat16
F32 = jnp.float32


def waves(rows, cols, length):
    turns = np.outer(rows, cols) % length
    angle = turns * (2.0 * math.pi / length)
    return np.cos(angle), np.sin(angle)


def tables():
    bf = np.dtype(BF16)
    every = np.arange(FA)
    cosine, sine = waves(every, every, FA)
    first = np.block([[cosine, -sine], [sine, cosine]]).astype(bf)
    half = np.arange(HALF)
    even_c, even_s = waves(half, 2 * half, FA)
    odd_c, odd_s = waves(half, 2 * half + 1, FA)
    second = np.stack(
        [
            np.block([[even_c, even_s], [-even_s, even_c]]),
            np.block([[odd_c, odd_s], [-odd_s, odd_c]]),
        ]
    ).astype(bf)
    coarse = np.block([[cosine, sine], [-sine, cosine]]).astype(np.float32)
    upper = coarse.astype(bf)
    lower = (coarse - upper.astype(np.float32)).astype(bf)
    turn = np.stack(waves(every, every, FA * FB)).astype(np.float32)
    return first, second, np.stack([upper, lower]), turn


def dot(left, right):
    return jnp.dot(left, right, preferred_element_type=F32)


def split(value):
    upper = value.astype(BF16)
    return upper, (value - upper.astype(F32)).astype(BF16)


def flip_orders(nseg):
    flips = [1 << k for k in range(1, nseg.bit_length() - 1)]
    return flips[::-1], flips


def reach(order, place):
    seg = 0
    for k, flip in enumerate(order):
        if place >> k & 1:
            seg ^= flip
    return seg


def filter_body(
    nseg, held, flips, live_ref, edges_ref, halves, slots, first_ref, second_ref, turn_ref,
    sums, tops, powers, lefts, spectra, products, firsts, turneds, series,
):
    orders = flip_orders(nseg)
    my_bank = lax.axis_index("bank")
    my_seg = lax.axis_index("seg")
    core = my_seg & 1
    rows = FB // nseg
    low = nseg // 2
    tiles = powers.shape[0] // len(flips)
    blocks = lax.broadcasted_iota(jnp.int32, (BINS, FB), 1)
    bins = lax.broadcasted_iota(jnp.int32, (BINS, FB), 0)

    def stage(n):
        q, k = n // tiles, n % tiles
        left, spectrum = lefts[n % 2], spectra[n % 2]
        t = owner(my_bank, core, flips[q]) * tiles + k
        (mine, mine_at), (theirs, theirs_at) = halves[q]
        for z in range(low):
            even, odd = reach(orders[0], z), reach(orders[1], z)
            own = my_seg ^ jnp.where(core == 0, even, odd)
            other = my_seg ^ 1 ^ jnp.where(core == 0, odd, even)
            for ref, at, seg in ((mine, mine_at, own), (theirs, theirs_at, other)):
                start = pl.multiple_of(seg * rows, rows)
                spectrum[:, pl.ds(start, rows), :] = ref[(at + z) * tiles + k].astype(F32)
        label = jnp.zeros((BINS, FB), jnp.int32)
        for j in range(BINS - 1):
            label = label + (edges_ref[t, j] <= blocks).astype(jnp.int32)
        onehot = (label == bins).astype(F32).astype(BF16)
        nothing = jnp.zeros((BINS, FB), BF16)
        left[0 : 2 * FB] = first_ref[...]
        left[2 * FB : 2 * FB + BINS, 0:FB] = onehot
        left[2 * FB : 2 * FB + BINS, FB:] = nothing
        left[2 * FB + BINS :, 0:FB] = nothing
        left[2 * FB + BINS :, FB:] = onehot
        energy = spectrum[0] * spectrum[0] + spectrum[1] * spectrum[1]
        energy = energy[:, :HALF] + energy[:, HALF:]
        upper, lower = split(energy)
        powers[n] = dot(onehot, upper) + dot(onehot, lower)

    def multiply(u):
        n, s = u // held, u % held
        spectrum = spectra[n % 2]
        for r in range(0, FB, STEP):
            lines = slice(r, r + STEP)
            hre, him = spectrum[0, lines], spectrum[1, lines]
            for d in range(2):
                sre = slots[s][d, 0, lines].astype(F32)
                sim = slots[s][d, 1, lines].astype(F32)
                product = products[u % 2 * 2 + d]
                product[lines] = (sre * hre + sim * him).astype(BF16)
                product[FB + r : FB + r + STEP] = (sim * hre - sre * him).astype(BF16)

    def transform(u, d):
        at = u % 2 * 2 + d
        firsts[at][...] = dot(lefts[u // held % 2][...], products[at][...])

    def turn_round(u, d):
        first, turned = firsts[u % 2 * 2 + d], turneds[u % 2 * 2 + d]
        for r in range(0, FB, STEP):
            out = slice(r, r + STEP)
            are, aim = first[out], first[FB + r : FB + r + STEP]
            cos, sin = turn_ref[0, out], turn_ref[1, out]
            bre = are * cos - aim * sin
            bim = are * sin + aim * cos
            turned[0, out, 0:HALF] = (bre[:, :HALF] + bre[:, HALF:]).astype(BF16)
            turned[0, out, HALF:] = (bim[:, :HALF] + bim[:, HALF:]).astype(BF16)
            turned[1, out, 0:HALF] = (bre[:, :HALF] - bre[:, HALF:]).astype(BF16)
            turned[1, out, HALF:] = (bim[:, :HALF] - bim[:, HALF:]).astype(BF16)
        base = (u * 2 + d) * BINS
        sums[base : base + BINS, 0:FA] = first[2 * FB : 2 * FB + BINS]
        sums[base : base + BINS, FA:] = first[2 * FB + BINS :]

    def finish(u, d):
        at = u % 2 * 2 + d
        for parity in range(2):
            series[at][parity] = dot(turneds[at][parity], second_ref[parity])

    def highest(u):
        best = None
        ones, twos = series[u % 2 * 2], series[u % 2 * 2 + 1]
        for parity in range(2):
            for r in range(0, FB, STEP):
                one, two = ones[parity, r : r + STEP], twos[parity, r : r + STEP]
                both = one * one + two * two
                both = both[:, :HALF] + both[:, HALF:]
                best = both if best is None else jnp.maximum(best, both)
        tops[u] = best

    units = powers.shape[0] * held
    stage(0)
    multiply(0)
    transform(0, 0)
    transform(0, 1)
    for u in range(units):
        more = u + 1 < units
        if more:
            if (u + 1) % held == 0:
                stage((u + 1) // held)
            multiply(u + 1)
        turn_round(u, 0)
        if more:
            transform(u + 1, 0)
        finish(u, 0)
        turn_round(u, 1)
        if more:
            transform(u + 1, 1)
        if u > 0:
            highest(u - 1)
        finish(u, 1)
    highest(units - 1)


def owner(my_bank, core, flip):
    return my_bank ^ (flip[0] if flip[0] == flip[1] else jnp.where(core == 0, flip[0], flip[1]))


def statistics(
    held, flips, live_ref, coarse_ref, groups, peak_ref, snr_ref, chi_ref, gathered, parts
):
    my_bank = lax.axis_index("bank")
    core = lax.axis_index("seg") & 1
    tiles = peak_ref.shape[1] // len(flips)
    at = 0
    for sums, _, _ in groups:
        gathered[at : at + sums.shape[0]] = sums[...]
        at += sums.shape[0]
    upper, lower = split(gathered[...])
    parts[...] = dot(upper, coarse_ref[0]) + dot(lower, coarse_ref[0]) + dot(upper, coarse_ref[1])
    peaks = jnp.zeros(peak_ref.shape, F32)
    slot_at = lax.broadcasted_iota(jnp.int32, peak_ref.shape, 0)
    tile_at = lax.broadcasted_iota(jnp.int32, peak_ref.shape, 1)
    n = 0
    for _, tops, powers in groups:
        for k in range(powers.shape[0]):
            t = owner(my_bank, core, flips[n // tiles]) * tiles + n % tiles
            hpower = jnp.sum(powers[k], axis=1, keepdims=True)
            sigma = jnp.sum(hpower, axis=0, keepdims=True)
            share = hpower / sigma
            for s in range(held):
                live = live_ref[s] != 0
                base = (n * held + s) * 2 * BINS
                snr = jnp.zeros((1, FB), F32)
                chi = jnp.zeros((1, FB), F32)
                for d in range(2):
                    own = parts[base + d * BINS : base + (d + 1) * BINS]
                    whole = jnp.sum(own, axis=0, keepdims=True)
                    diff = own - share * whole
                    diff = jnp.sum(diff * diff, axis=0, keepdims=True)
                    whole = whole * whole
                    snr = snr + whole[:, :FB] + whole[:, FB:]
                    chi = chi + diff[:, :FB] + diff[:, FB:]
                snr_ref[t, s : s + 1] = jnp.where(live, snr / sigma, 0.0)
                chi = chi / sigma / (4.0 * (BINS - 1))
                chi_ref[t, s : s + 1] = jnp.where(live, chi, 0.0)
                top = jnp.max(tops[k * held + s], axis=0, keepdims=True)
                top = jnp.sqrt(jnp.max(top, axis=1, keepdims=True) / sigma)
                peaks = jnp.where((slot_at == s) & (tile_at == t) & live, top, peaks)
            n += 1
    peak_ref[...] = peaks


def on_device(nbank, nseg, strain, templates, bin_edges, live_flags):
    held = strain.shape[0]
    tiles = templates.shape[0]
    total = tiles * nbank
    rows = FB // nseg
    low = nseg // 2
    first, second, coarse, turn = (jnp.asarray(x) for x in tables())
    orders = flip_orders(nseg)
    smem = pl.BlockSpec(memory_space=pltpu.SMEM)
    vmem = pl.BlockSpec(memory_space=pltpu.VMEM)

    def swap(block, flips):
        route = []
        for b in range(nbank):
            for s in range(nseg):
                flip_bank, flip_seg = flips[s & 1]
                route.append((b * nseg + s, (b ^ flip_bank) * nseg + (s ^ flip_seg)))
        return lax.ppermute(block, ("bank", "seg"), route)

    twin = ((0, 1), (0, 1))

    def call(flips, arrays, halves, earlier=None):
        fresh = len(flips) * tiles
        made = [
            jax.ShapeDtypeStruct((fresh * held * 2 * BINS, 2 * FA), F32),
            jax.ShapeDtypeStruct((fresh * held, STEP, HALF), F32),
            jax.ShapeDtypeStruct((fresh, BINS, HALF), F32),
        ]
        scratch = [
            [pltpu.VMEM((2 * FB + 2 * BINS, 2 * FB), BF16) for _ in range(2)],
            [pltpu.VMEM((2, FB, FA), F32) for _ in range(2)],
            [pltpu.VMEM((2 * FB, FA), BF16) for _ in range(4)],
            [pltpu.VMEM((2 * FB + 2 * BINS, FA), F32) for _ in range(4)],
            [pltpu.VMEM((2, FB, FA), BF16) for _ in range(4)],
            [pltpu.VMEM((2, FB, FA), F32) for _ in range(4)],
        ]
        count = len(arrays)

        def run(live_ref, edges_ref, first_ref, second_ref, turn_ref, *rest):
            slots, rest = rest[:held], rest[held:]
            spectra, rest = rest[:count], rest[count:]
            pairs = [[(spectra[i], at) for i, at in half] for half in halves]
            if earlier is None:
                results, scratches = rest[:3], rest[3:]
            else:
                coarse_ref, rest = rest[0], rest[1:]
                groups = [rest[i : i + 3] for i in range(0, 3 * len(earlier[1]), 3)]
                rest = rest[3 * len(groups) :]
                outs, results, scratches = rest[:3], rest[3:6], rest[8:]
            filter_body(
                nseg, held, flips, live_ref, edges_ref, pairs, slots,
                first_ref, second_ref, turn_ref, *results, *scratches,
            )
            if earlier is not None:
                every = earlier[0] + flips
                groups = groups + [results]
                statistics(held, every, live_ref, coarse_ref, groups, *outs, *rest[6:8])

        inputs = [live_flags, bin_edges, first, second, turn, *slots, *arrays]
        if earlier is None:
            shapes = made
        else:
            inputs += [coarse] + [x for group in earlier[1] for x in group]
            shapes = [
                jax.ShapeDtypeStruct((held, total), F32),
                jax.ShapeDtypeStruct((total, held, FB), F32),
                jax.ShapeDtypeStruct((total, held, FB), F32),
            ]
            full = pltpu.VMEM((total * held * 2 * BINS, 2 * FA), F32)
            scratch = [pltpu.VMEM(x.shape, x.dtype) for x in made] + [full, full] + scratch
        return pl.pallas_call(
            run,
            in_specs=[smem, smem] + [vmem] * (len(inputs) - 2),
            out_specs=[vmem] * 3,
            out_shape=shapes,
            scratch_shapes=scratch,
            compiler_params=pltpu.CompilerParams(vmem_limit_bytes=24 << 20),
            cost_estimate=pl.CostEstimate(
                flops=1 * fresh * held * 2 * 12 * FA**3, bytes_accessed=1 << 20, transcendentals=0
            ),
        )(*inputs)

    block = templates.reshape(tiles, 2, rows, FA)
    slots = []
    for step in range(len(orders[0])):
        found = swap(block, [(0, orders[c][step]) for c in range(2)])
        if step < held:
            slot = strain[step].reshape(2, 2, FB, FA)
            found, slot = lax.optimization_barrier((found, slot))
            slots.append(slot)
        block = jnp.concatenate([block, found], axis=0)
    for s in range(len(slots), held):
        slots.append(strain[s].reshape(2, 2, FB, FA))
    other = swap(block, twin)
    corner = swap(block, ((3, 0), (3, 0)))
    side = swap(jnp.concatenate([block, other], axis=0), ((1, 0), (2, 0)))
    here = call([(0, 0)], [block, other], [((0, 0), (1, 0))])
    side, corner, here = lax.optimization_barrier((side, corner, here))
    far = swap(side, twin)
    other_corner = swap(corner, twin)
    beside = call([(1, 2)], [side], [((0, 0), (0, low))])
    far, other_corner, beside = lax.optimization_barrier((far, other_corner, beside))
    peak, snr, chi = call(
        [(2, 1), (3, 3)],
        [far, corner, other_corner],
        [((0, low), (0, 0)), ((1, 0), (2, 0))],
        ([(0, 0), (1, 2)], [here, beside]),
    )
    return peak.T, snr, chi


def solution(mesh):
    in_specs = (
        P(("bank", "seg"), None, None, None),
        P("bank", None, "seg"),
        P(),
        P(("bank", "seg")),
    )
    out_specs = (
        P(None, ("bank", "seg")),
        P(None, ("bank", "seg"), None),
        P(None, ("bank", "seg"), None),
    )
    body = functools.partial(on_device, mesh.shape["bank"], mesh.shape["seg"])
    return jax.shard_map(body, mesh=mesh, in_specs=in_specs, out_specs=out_specs, check_vma=False)
```

```python
import functools
import math

import jax
import jax.numpy as jnp
import numpy as np
from jax import lax
from jax.experimental import pallas as pl
from jax.experimental.pallas import tpu as pltpu
from jax.sharding import PartitionSpec as P

FA = 256
FB = 256
HALF = 128
BINS = 16
STEP = 16
BF16 = jnp.bfloat16
F32 = jnp.float32


def waves(rows, cols, length):
    turns = np.outer(rows, cols) % length
    angle = turns * (2.0 * math.pi / length)
    return np.cos(angle), np.sin(angle)


def tables():
    bf = np.dtype(BF16)
    every = np.arange(FA)
    cosine, sine = waves(every, every, FA)
    first = np.block([[cosine, -sine], [sine, cosine]]).astype(bf)
    half = np.arange(HALF)
    even_c, even_s = waves(half, 2 * half, FA)
    odd_c, odd_s = waves(half, 2 * half + 1, FA)
    second = np.stack(
        [
            np.block([[even_c, even_s], [-even_s, even_c]]),
            np.block([[odd_c, odd_s], [-odd_s, odd_c]]),
        ]
    ).astype(bf)
    coarse = np.block([[cosine, sine], [-sine, cosine]]).astype(np.float32)
    upper = coarse.astype(bf)
    lower = (coarse - upper.astype(np.float32)).astype(bf)
    turn = np.stack(waves(every, every, FA * FB)).astype(np.float32)
    return first, second, np.stack([upper, lower]), turn


def dot(left, right):
    return jnp.dot(left, right, preferred_element_type=F32)


def split(value):
    upper = value.astype(BF16)
    return upper, (value - upper.astype(F32)).astype(BF16)


def flip_orders(nseg):
    flips = [1 << k for k in range(1, nseg.bit_length() - 1)]
    return flips[::-1], flips


def reach(order, place):
    seg = 0
    for k, flip in enumerate(order):
        if place >> k & 1:
            seg ^= flip
    return seg


def filter_body(
    nseg, held, flips, live_ref, edges_ref, halves, slots, first_ref, second_ref, turn_ref,
    sums, tops, powers, lefts, spectra, products, firsts, turneds, series,
):
    orders = flip_orders(nseg)
    my_bank = lax.axis_index("bank")
    my_seg = lax.axis_index("seg")
    core = my_seg & 1
    rows = FB // nseg
    low = nseg // 2
    tiles = powers.shape[0] // len(flips)
    blocks = lax.broadcasted_iota(jnp.int32, (BINS, FB), 1)
    bins = lax.broadcasted_iota(jnp.int32, (BINS, FB), 0)

    def stage(n):
        q, k = n // tiles, n % tiles
        left, spectrum = lefts[n % 2], spectra[n % 2]
        t = owner(my_bank, core, flips[q]) * tiles + k
        (mine, mine_at), (theirs, theirs_at) = halves[q]
        for z in range(low):
            even, odd = reach(orders[0], z), reach(orders[1], z)
            own = my_seg ^ jnp.where(core == 0, even, odd)
            other = my_seg ^ 1 ^ jnp.where(core == 0, odd, even)
            for ref, at, seg in ((mine, mine_at, own), (theirs, theirs_at, other)):
                start = pl.multiple_of(seg * rows, rows)
                spectrum[:, pl.ds(start, rows), :] = ref[(at + z) * tiles + k].astype(F32)
        label = jnp.zeros((BINS, FB), jnp.int32)
        for j in range(BINS - 1):
            label = label + (edges_ref[t, j] <= blocks).astype(jnp.int32)
        onehot = (label == bins).astype(F32).astype(BF16)
        nothing = jnp.zeros((BINS, FB), BF16)
        left[0 : 2 * FB] = first_ref[...]
        left[2 * FB : 2 * FB + BINS, 0:FB] = onehot
        left[2 * FB : 2 * FB + BINS, FB:] = nothing
        left[2 * FB + BINS :, 0:FB] = nothing
        left[2 * FB + BINS :, FB:] = onehot
        energy = spectrum[0] * spectrum[0] + spectrum[1] * spectrum[1]
        energy = energy[:, :HALF] + energy[:, HALF:]
        upper, lower = split(energy)
        powers[n] = dot(onehot, upper) + dot(onehot, lower)

    def multiply(u):
        n, s = u // held, u % held
        spectrum = spectra[n % 2]
        for r in range(0, FB, STEP):
            lines = slice(r, r + STEP)
            hre, him = spectrum[0, lines], spectrum[1, lines]
            for d in range(2):
                sre = slots[s][d, 0, lines].astype(F32)
                sim = slots[s][d, 1, lines].astype(F32)
                product = products[u % 2 * 2 + d]
                product[lines] = (sre * hre + sim * him).astype(BF16)
                product[FB + r : FB + r + STEP] = (sim * hre - sre * him).astype(BF16)

    def transform(u, d):
        at = u % 2 * 2 + d
        firsts[at][...] = dot(lefts[u // held % 2][...], products[at][...])

    def turn_round(u, d):
        first, turned = firsts[u % 2 * 2 + d], turneds[u % 2 * 2 + d]
        for r in range(0, FB, STEP):
            out = slice(r, r + STEP)
            are, aim = first[out], first[FB + r : FB + r + STEP]
            cos, sin = turn_ref[0, out], turn_ref[1, out]
            bre = are * cos - aim * sin
            bim = are * sin + aim * cos
            turned[0, out, 0:HALF] = (bre[:, :HALF] + bre[:, HALF:]).astype(BF16)
            turned[0, out, HALF:] = (bim[:, :HALF] + bim[:, HALF:]).astype(BF16)
            turned[1, out, 0:HALF] = (bre[:, :HALF] - bre[:, HALF:]).astype(BF16)
            turned[1, out, HALF:] = (bim[:, :HALF] - bim[:, HALF:]).astype(BF16)
        base = (u * 2 + d) * BINS
        sums[base : base + BINS, 0:FA] = first[2 * FB : 2 * FB + BINS]
        sums[base : base + BINS, FA:] = first[2 * FB + BINS :]

    def finish(u, d):
        at = u % 2 * 2 + d
        for parity in range(2):
            series[at][parity] = dot(turneds[at][parity], second_ref[parity])

    def highest(u):
        best = None
        ones, twos = series[u % 2 * 2], series[u % 2 * 2 + 1]
        for parity in range(2):
            for r in range(0, FB, STEP):
                one, two = ones[parity, r : r + STEP], twos[parity, r : r + STEP]
                both = one * one + two * two
                both = both[:, :HALF] + both[:, HALF:]
                best = both if best is None else jnp.maximum(best, both)
        tops[u] = best

    units = powers.shape[0] * held
    stage(0)
    multiply(0)
    transform(0, 0)
    transform(0, 1)
    for u in range(units):
        more = u + 1 < units
        if more:
            if (u + 1) % held == 0:
                stage((u + 1) // held)
            multiply(u + 1)
        turn_round(u, 0)
        if more:
            transform(u + 1, 0)
        finish(u, 0)
        turn_round(u, 1)
        if more:
            transform(u + 1, 1)
        if u > 0:
            highest(u - 1)
        finish(u, 1)
    highest(units - 1)


def owner(my_bank, core, flip):
    return my_bank ^ (flip[0] if flip[0] == flip[1] else jnp.where(core == 0, flip[0], flip[1]))


def statistics(
    held, flips, live_ref, coarse_ref, groups, peak_ref, snr_ref, chi_ref, gathered, parts
):
    my_bank = lax.axis_index("bank")
    core = lax.axis_index("seg") & 1
    tiles = peak_ref.shape[1] // len(flips)
    at = 0
    for sums, _, _ in groups:
        gathered[at : at + sums.shape[0]] = sums[...]
        at += sums.shape[0]
    upper, lower = split(gathered[...])
    parts[...] = dot(upper, coarse_ref[0]) + dot(lower, coarse_ref[0]) + dot(upper, coarse_ref[1])
    peaks = jnp.zeros(peak_ref.shape, F32)
    slot_at = lax.broadcasted_iota(jnp.int32, peak_ref.shape, 0)
    tile_at = lax.broadcasted_iota(jnp.int32, peak_ref.shape, 1)
    n = 0
    for _, tops, powers in groups:
        for k in range(powers.shape[0]):
            t = owner(my_bank, core, flips[n // tiles]) * tiles + n % tiles
            hpower = jnp.sum(powers[k], axis=1, keepdims=True)
            sigma = jnp.sum(hpower, axis=0, keepdims=True)
            share = hpower / sigma
            for s in range(held):
                live = live_ref[s] != 0
                base = (n * held + s) * 2 * BINS
                snr = jnp.zeros((1, FB), F32)
                chi = jnp.zeros((1, FB), F32)
                for d in range(2):
                    own = parts[base + d * BINS : base + (d + 1) * BINS]
                    whole = jnp.sum(own, axis=0, keepdims=True)
                    diff = own - share * whole
                    diff = jnp.sum(diff * diff, axis=0, keepdims=True)
                    whole = whole * whole
                    snr = snr + whole[:, :FB] + whole[:, FB:]
                    chi = chi + diff[:, :FB] + diff[:, FB:]
                snr_ref[t, s : s + 1] = jnp.where(live, snr / sigma, 0.0)
                chi = chi / sigma / (4.0 * (BINS - 1))
                chi_ref[t, s : s + 1] = jnp.where(live, chi, 0.0)
                top = jnp.max(tops[k * held + s], axis=0, keepdims=True)
                top = jnp.sqrt(jnp.max(top, axis=1, keepdims=True) / sigma)
                peaks = jnp.where((slot_at == s) & (tile_at == t) & live, top, peaks)
            n += 1
    peak_ref[...] = peaks


def on_device(nbank, nseg, strain, templates, bin_edges, live_flags):
    held = strain.shape[0]
    tiles = templates.shape[0]
    total = tiles * nbank
    rows = FB // nseg
    low = nseg // 2
    first, second, coarse, turn = (jnp.asarray(x) for x in tables())
    orders = flip_orders(nseg)
    smem = pl.BlockSpec(memory_space=pltpu.SMEM)
    vmem = pl.BlockSpec(memory_space=pltpu.VMEM)

    def swap(block, flips):
        route = []
        for b in range(nbank):
            for s in range(nseg):
                flip_bank, flip_seg = flips[s & 1]
                route.append((b * nseg + s, (b ^ flip_bank) * nseg + (s ^ flip_seg)))
        return lax.ppermute(block, ("bank", "seg"), route)

    twin = ((0, 1), (0, 1))

    def call(flips, arrays, halves, earlier=None):
        fresh = len(flips) * tiles
        made = [
            jax.ShapeDtypeStruct((fresh * held * 2 * BINS, 2 * FA), F32),
            jax.ShapeDtypeStruct((fresh * held, STEP, HALF), F32),
            jax.ShapeDtypeStruct((fresh, BINS, HALF), F32),
        ]
        scratch = [
            [pltpu.VMEM((2 * FB + 2 * BINS, 2 * FB), BF16) for _ in range(2)],
            [pltpu.VMEM((2, FB, FA), F32) for _ in range(2)],
            [pltpu.VMEM((2 * FB, FA), BF16) for _ in range(4)],
            [pltpu.VMEM((2 * FB + 2 * BINS, FA), F32) for _ in range(4)],
            [pltpu.VMEM((2, FB, FA), BF16) for _ in range(4)],
            [pltpu.VMEM((2, FB, FA), F32) for _ in range(4)],
        ]
        count = len(arrays)

        def run(live_ref, edges_ref, first_ref, second_ref, turn_ref, *rest):
            slots, rest = rest[:held], rest[held:]
            spectra, rest = rest[:count], rest[count:]
            pairs = [[(spectra[i], at) for i, at in half] for half in halves]
            if earlier is None:
                results, scratches = rest[:3], rest[3:]
            else:
                coarse_ref, rest = rest[0], rest[1:]
                groups = [rest[i : i + 3] for i in range(0, 3 * len(earlier[1]), 3)]
                rest = rest[3 * len(groups) :]
                outs, results, scratches = rest[:3], rest[3:6], rest[8:]
            filter_body(
                nseg, held, flips, live_ref, edges_ref, pairs, slots,
                first_ref, second_ref, turn_ref, *results, *scratches,
            )
            if earlier is not None:
                every = earlier[0] + flips
                groups = groups + [results]
                statistics(held, every, live_ref, coarse_ref, groups, *outs, *rest[6:8])

        inputs = [live_flags, bin_edges, first, second, turn, *slots, *arrays]
        if earlier is None:
            shapes = made
        else:
            inputs += [coarse] + [x for group in earlier[1] for x in group]
            shapes = [
                jax.ShapeDtypeStruct((held, total), F32),
                jax.ShapeDtypeStruct((total, held, FB), F32),
                jax.ShapeDtypeStruct((total, held, FB), F32),
            ]
            full = pltpu.VMEM((total * held * 2 * BINS, 2 * FA), F32)
            scratch = [pltpu.VMEM(x.shape, x.dtype) for x in made] + [full, full] + scratch
        return pl.pallas_call(
            run,
            in_specs=[smem, smem] + [vmem] * (len(inputs) - 2),
            out_specs=[vmem] * 3,
            out_shape=shapes,
            scratch_shapes=scratch,
            compiler_params=pltpu.CompilerParams(vmem_limit_bytes=24 << 20),
            cost_estimate=pl.CostEstimate(
                flops=1 * fresh * held * 2 * 12 * FA**3, bytes_accessed=1 << 20, transcendentals=0
            ),
        )(*inputs)

    block = templates.reshape(tiles, 2, rows, FA)
    slots = []
    for step in range(len(orders[0])):
        found = swap(block, [(0, orders[c][step]) for c in range(2)])
        if step < held:
            slot = strain[step].reshape(2, 2, FB, FA)
            found, slot, strain = lax.optimization_barrier((found, slot, strain))
            slots.append(slot)
        block = jnp.concatenate([block, found], axis=0)
    for s in range(len(slots), held):
        slots.append(strain[s].reshape(2, 2, FB, FA))
    other = swap(block, twin)
    side = swap(jnp.concatenate([block, other], axis=0), ((1, 0), (2, 0)))
    here = call([(0, 0)], [block, other], [((0, 0), (1, 0))])
    side, here = lax.optimization_barrier((side, here))
    corner = swap(side[: low * tiles], ((2, 0), (1, 0)))
    far = swap(side, twin)
    beside = call([(1, 2)], [side], [((0, 0), (0, low))])
    corner, beside = lax.optimization_barrier((corner, beside))
    other_corner = swap(corner, twin)
    across = call([(2, 1)], [far], [((0, low), (0, 0))])
    other_corner, across = lax.optimization_barrier((other_corner, across))
    peak, snr, chi = call(
        [(3, 3)],
        [corner, other_corner],
        [((0, 0), (1, 0))],
        ([(0, 0), (1, 2), (2, 1)], [here, beside, across]),
    )
    return peak.T, snr, chi


def solution(mesh):
    in_specs = (
        P(("bank", "seg"), None, None, None),
        P("bank", None, "seg"),
        P(),
        P(("bank", "seg")),
    )
    out_specs = (
        P(None, ("bank", "seg")),
        P(None, ("bank", "seg"), None),
        P(None, ("bank", "seg"), None),
    )
    body = functools.partial(on_device, mesh.shape["bank"], mesh.shape["seg"])
    return jax.shard_map(body, mesh=mesh, in_specs=in_specs, out_specs=out_specs, check_vma=False)
```

```python
import functools
import math

import jax
import jax.numpy as jnp
import numpy as np
from jax import lax
from jax.experimental import pallas as pl
from jax.experimental.pallas import tpu as pltpu
from jax.sharding import PartitionSpec as P

FA = 256
FB = 256
HALF = 128
BINS = 16
STEP = 16
BF16 = jnp.bfloat16
F32 = jnp.float32


def waves(rows, cols, length):
    turns = np.outer(rows, cols) % length
    angle = turns * (2.0 * math.pi / length)
    return np.cos(angle), np.sin(angle)


def tables():
    bf = np.dtype(BF16)
    every = np.arange(FA)
    cosine, sine = waves(every, every, FA)
    first = np.block([[cosine, -sine], [sine, cosine]]).astype(bf)
    half = np.arange(HALF)
    even_c, even_s = waves(half, 2 * half, FA)
    odd_c, odd_s = waves(half, 2 * half + 1, FA)
    second = np.stack(
        [
            np.block([[even_c, even_s], [-even_s, even_c]]),
            np.block([[odd_c, odd_s], [-odd_s, odd_c]]),
        ]
    ).astype(bf)
    coarse = np.block([[cosine, sine], [-sine, cosine]]).astype(np.float32)
    upper = coarse.astype(bf)
    lower = (coarse - upper.astype(np.float32)).astype(bf)
    turn = np.stack(waves(every, every, FA * FB)).astype(np.float32)
    return first, second, np.stack([upper, lower]), turn


def dot(left, right):
    return jnp.dot(left, right, preferred_element_type=F32)


def split(value):
    upper = value.astype(BF16)
    return upper, (value - upper.astype(F32)).astype(BF16)


def doublings(nseg):
    flips = [1 << k for k in range(1, nseg.bit_length() - 1)]
    return flips[::-1], flips


def holdings(nseg):
    if nseg == 8:
        return [0, 6, 2, 3], [0, 6, 4, 5]
    held = []
    for order in doublings(nseg):
        flips = [0]
        for flip in order:
            flips = flips + [x ^ flip for x in flips]
        held.append(flips)
    return held


def filter_body(
    nseg, held, flips, live_ref, edges_ref, halves, slots, first_ref, second_ref, turn_ref,
    sums, tops, powers, lefts, spectra, products, firsts, turneds, series,
):
    evens, odds = holdings(nseg)
    my_bank = lax.axis_index("bank")
    my_seg = lax.axis_index("seg")
    core = my_seg & 1
    rows = FB // nseg
    low = nseg // 2
    tiles = powers.shape[0] // len(flips)
    blocks = lax.broadcasted_iota(jnp.int32, (BINS, FB), 1)
    bins = lax.broadcasted_iota(jnp.int32, (BINS, FB), 0)

    def stage(n):
        q, k = n // tiles, n % tiles
        left, spectrum = lefts[n % 2], spectra[n % 2]
        t = owner(my_bank, core, flips[q]) * tiles + k
        (mine, mine_at), (theirs, theirs_at) = halves[q]
        for z in range(low):
            even, odd = evens[z], odds[z]
            own = my_seg ^ jnp.where(core == 0, even, odd)
            other = my_seg ^ 1 ^ jnp.where(core == 0, odd, even)
            for ref, at, seg in ((mine, mine_at, own), (theirs, theirs_at, other)):
                start = pl.multiple_of(seg * rows, rows)
                spectrum[:, pl.ds(start, rows), :] = ref[(at + z) * tiles + k].astype(F32)
        label = jnp.zeros((BINS, FB), jnp.int32)
        for j in range(BINS - 1):
            label = label + (edges_ref[t, j] <= blocks).astype(jnp.int32)
        onehot = (label == bins).astype(F32).astype(BF16)
        nothing = jnp.zeros((BINS, FB), BF16)
        left[0 : 2 * FB] = first_ref[...]
        left[2 * FB : 2 * FB + BINS, 0:FB] = onehot
        left[2 * FB : 2 * FB + BINS, FB:] = nothing
        left[2 * FB + BINS :, 0:FB] = nothing
        left[2 * FB + BINS :, FB:] = onehot
        energy = spectrum[0] * spectrum[0] + spectrum[1] * spectrum[1]
        energy = energy[:, :HALF] + energy[:, HALF:]
        upper, lower = split(energy)
        powers[n] = dot(onehot, upper) + dot(onehot, lower)

    def multiply(u):
        n, s = u // held, u % held
        spectrum = spectra[n % 2]
        for r in range(0, FB, STEP):
            lines = slice(r, r + STEP)
            hre, him = spectrum[0, lines], spectrum[1, lines]
            for d in range(2):
                sre = slots[s][d, 0, lines].astype(F32)
                sim = slots[s][d, 1, lines].astype(F32)
                product = products[u % 2 * 2 + d]
                product[lines] = (sre * hre + sim * him).astype(BF16)
                product[FB + r : FB + r + STEP] = (sim * hre - sre * him).astype(BF16)

    def transform(u, d):
        at = u % 2 * 2 + d
        firsts[at][...] = dot(lefts[u // held % 2][...], products[at][...])

    def turn_round(u, d):
        first, turned = firsts[u % 2 * 2 + d], turneds[u % 2 * 2 + d]
        for r in range(0, FB, STEP):
            out = slice(r, r + STEP)
            are, aim = first[out], first[FB + r : FB + r + STEP]
            cos, sin = turn_ref[0, out], turn_ref[1, out]
            bre = are * cos - aim * sin
            bim = are * sin + aim * cos
            turned[0, out, 0:HALF] = (bre[:, :HALF] + bre[:, HALF:]).astype(BF16)
            turned[0, out, HALF:] = (bim[:, :HALF] + bim[:, HALF:]).astype(BF16)
            turned[1, out, 0:HALF] = (bre[:, :HALF] - bre[:, HALF:]).astype(BF16)
            turned[1, out, HALF:] = (bim[:, :HALF] - bim[:, HALF:]).astype(BF16)
        base = (u * 2 + d) * BINS
        sums[base : base + BINS, 0:FA] = first[2 * FB : 2 * FB + BINS]
        sums[base : base + BINS, FA:] = first[2 * FB + BINS :]

    def finish(u, d):
        at = u % 2 * 2 + d
        for parity in range(2):
            series[at][parity] = dot(turneds[at][parity], second_ref[parity])

    def highest(u):
        best = None
        ones, twos = series[u % 2 * 2], series[u % 2 * 2 + 1]
        for parity in range(2):
            for r in range(0, FB, STEP):
                one, two = ones[parity, r : r + STEP], twos[parity, r : r + STEP]
                both = one * one + two * two
                both = both[:, :HALF] + both[:, HALF:]
                best = both if best is None else jnp.maximum(best, both)
        tops[u] = best

    units = powers.shape[0] * held
    stage(0)
    multiply(0)
    transform(0, 0)
    transform(0, 1)
    for u in range(units):
        more = u + 1 < units
        if more:
            if (u + 1) % held == 0:
                stage((u + 1) // held)
            multiply(u + 1)
        turn_round(u, 0)
        if more:
            transform(u + 1, 0)
        finish(u, 0)
        turn_round(u, 1)
        if more:
            transform(u + 1, 1)
        if u > 0:
            highest(u - 1)
        finish(u, 1)
    highest(units - 1)


def owner(my_bank, core, flip):
    return my_bank ^ (flip[0] if flip[0] == flip[1] else jnp.where(core == 0, flip[0], flip[1]))


def statistics(
    held, flips, live_ref, coarse_ref, groups, peak_ref, snr_ref, chi_ref, gathered, parts
):
    my_bank = lax.axis_index("bank")
    core = lax.axis_index("seg") & 1
    tiles = peak_ref.shape[1] // len(flips)
    at = 0
    for sums, _, _ in groups:
        gathered[at : at + sums.shape[0]] = sums[...]
        at += sums.shape[0]
    upper, lower = split(gathered[...])
    parts[...] = dot(upper, coarse_ref[0]) + dot(lower, coarse_ref[0]) + dot(upper, coarse_ref[1])
    peaks = jnp.zeros(peak_ref.shape, F32)
    slot_at = lax.broadcasted_iota(jnp.int32, peak_ref.shape, 0)
    tile_at = lax.broadcasted_iota(jnp.int32, peak_ref.shape, 1)
    n = 0
    for _, tops, powers in groups:
        for k in range(powers.shape[0]):
            t = owner(my_bank, core, flips[n // tiles]) * tiles + n % tiles
            hpower = jnp.sum(powers[k], axis=1, keepdims=True)
            sigma = jnp.sum(hpower, axis=0, keepdims=True)
            share = hpower / sigma
            for s in range(held):
                live = live_ref[s] != 0
                base = (n * held + s) * 2 * BINS
                snr = jnp.zeros((1, FB), F32)
                chi = jnp.zeros((1, FB), F32)
                for d in range(2):
                    own = parts[base + d * BINS : base + (d + 1) * BINS]
                    whole = jnp.sum(own, axis=0, keepdims=True)
                    diff = own - share * whole
                    diff = jnp.sum(diff * diff, axis=0, keepdims=True)
                    whole = whole * whole
                    snr = snr + whole[:, :FB] + whole[:, FB:]
                    chi = chi + diff[:, :FB] + diff[:, FB:]
                snr_ref[t, s : s + 1] = jnp.where(live, snr / sigma, 0.0)
                chi = chi / sigma / (4.0 * (BINS - 1))
                chi_ref[t, s : s + 1] = jnp.where(live, chi, 0.0)
                top = jnp.max(tops[k * held + s], axis=0, keepdims=True)
                top = jnp.sqrt(jnp.max(top, axis=1, keepdims=True) / sigma)
                peaks = jnp.where((slot_at == s) & (tile_at == t) & live, top, peaks)
            n += 1
    peak_ref[...] = peaks


def on_device(nbank, nseg, strain, templates, bin_edges, live_flags):
    held = strain.shape[0]
    tiles = templates.shape[0]
    total = tiles * nbank
    rows = FB // nseg
    low = nseg // 2
    first, second, coarse, turn = (jnp.asarray(x) for x in tables())
    smem = pl.BlockSpec(memory_space=pltpu.SMEM)
    vmem = pl.BlockSpec(memory_space=pltpu.VMEM)

    def swap(block, flips):
        route = []
        for b in range(nbank):
            for s in range(nseg):
                flip_bank, flip_seg = flips[s & 1]
                route.append((b * nseg + s, (b ^ flip_bank) * nseg + (s ^ flip_seg)))
        return lax.ppermute(block, ("bank", "seg"), route)

    twin = ((0, 1), (0, 1))

    def call(flips, arrays, halves, earlier=None):
        fresh = len(flips) * tiles
        made = [
            jax.ShapeDtypeStruct((fresh * held * 2 * BINS, 2 * FA), F32),
            jax.ShapeDtypeStruct((fresh * held, STEP, HALF), F32),
            jax.ShapeDtypeStruct((fresh, BINS, HALF), F32),
        ]
        scratch = [
            [pltpu.VMEM((2 * FB + 2 * BINS, 2 * FB), BF16) for _ in range(2)],
            [pltpu.VMEM((2, FB, FA), F32) for _ in range(2)],
            [pltpu.VMEM((2 * FB, FA), BF16) for _ in range(4)],
            [pltpu.VMEM((2 * FB + 2 * BINS, FA), F32) for _ in range(4)],
            [pltpu.VMEM((2, FB, FA), BF16) for _ in range(4)],
            [pltpu.VMEM((2, FB, FA), F32) for _ in range(4)],
        ]
        count = len(arrays)

        def run(live_ref, edges_ref, first_ref, second_ref, turn_ref, *rest):
            slots, rest = rest[:held], rest[held:]
            spectra, rest = rest[:count], rest[count:]
            pairs = [[(spectra[i], at) for i, at in half] for half in halves]
            if earlier is None:
                results, scratches = rest[:3], rest[3:]
            else:
                coarse_ref, rest = rest[0], rest[1:]
                groups = [rest[i : i + 3] for i in range(0, 3 * len(earlier[1]), 3)]
                rest = rest[3 * len(groups) :]
                outs, results, scratches = rest[:3], rest[3:6], rest[8:]
            filter_body(
                nseg, held, flips, live_ref, edges_ref, pairs, slots,
                first_ref, second_ref, turn_ref, *results, *scratches,
            )
            if earlier is not None:
                every = earlier[0] + flips
                groups = groups + [results]
                statistics(held, every, live_ref, coarse_ref, groups, *outs, *rest[6:8])

        inputs = [live_flags, bin_edges, first, second, turn, *slots, *arrays]
        if earlier is None:
            shapes = made
        else:
            inputs += [coarse] + [x for group in earlier[1] for x in group]
            shapes = [
                jax.ShapeDtypeStruct((held, total), F32),
                jax.ShapeDtypeStruct((total, held, FB), F32),
                jax.ShapeDtypeStruct((total, held, FB), F32),
            ]
            full = pltpu.VMEM((total * held * 2 * BINS, 2 * FA), F32)
            scratch = [pltpu.VMEM(x.shape, x.dtype) for x in made] + [full, full] + scratch
        return pl.pallas_call(
            run,
            in_specs=[smem, smem] + [vmem] * (len(inputs) - 2),
            out_specs=[vmem] * 3,
            out_shape=shapes,
            scratch_shapes=scratch,
            compiler_params=pltpu.CompilerParams(vmem_limit_bytes=24 << 20),
            cost_estimate=pl.CostEstimate(
                flops=1 * fresh * held * 2 * 12 * FA**3, bytes_accessed=1 << 20, transcendentals=0
            ),
        )(*inputs)

    block = templates.reshape(tiles, 2, rows, FA)
    slots = []

    def slot_beside(found, strain):
        slot = strain[len(slots)].reshape(2, 2, FB, FA)
        found, slot, strain = lax.optimization_barrier((found, slot, strain))
        slots.append(slot)
        return found, strain

    if nseg == 8:
        pair = jnp.concatenate([block, swap(block, twin)], axis=0)
        third = swap(block, ((0, 6), (0, 6)))
        near = swap(pair, ((0, 2), (0, 4)))
        near, strain = slot_beside(near, strain)
        block = jnp.concatenate([block, third, near], axis=0)
    else:
        for even, odd in zip(*doublings(nseg)):
            found = swap(block, ((0, even), (0, odd)))
            if len(slots) < held:
                found, strain = slot_beside(found, strain)
            block = jnp.concatenate([block, found], axis=0)
    other = swap(block, twin)
    one = swap(block, ((1, 0), (2, 0)))
    two = swap(block, ((2, 0), (1, 0)))
    while len(slots) < held:
        slots.append(strain[len(slots)].reshape(2, 2, FB, FA))
    here = call([(0, 0)], [block, other], [((0, 0), (1, 0))])
    one, two, here = lax.optimization_barrier((one, two, here))
    others = swap(jnp.concatenate([one, two], axis=0), twin)
    corner = swap(one, ((2, 0), (1, 0)))
    beside = call([(1, 2)], [one, others], [((0, 0), (1, low))])
    corner, beside = lax.optimization_barrier((corner, beside))
    other_corner = swap(corner, twin)
    across = call([(2, 1)], [two, others], [((0, 0), (1, 0))])
    other_corner, across = lax.optimization_barrier((other_corner, across))
    peak, snr, chi = call(
        [(3, 3)],
        [corner, other_corner],
        [((0, 0), (1, 0))],
        ([(0, 0), (1, 2), (2, 1)], [here, beside, across]),
    )
    return peak.T, snr, chi


def solution(mesh):
    in_specs = (
        P(("bank", "seg"), None, None, None),
        P("bank", None, "seg"),
        P(),
        P(("bank", "seg")),
    )
    out_specs = (
        P(None, ("bank", "seg")),
        P(None, ("bank", "seg"), None),
        P(None, ("bank", "seg"), None),
    )
    body = functools.partial(on_device, mesh.shape["bank"], mesh.shape["seg"])
    return jax.shard_map(body, mesh=mesh, in_specs=in_specs, out_specs=out_specs, check_vma=False)
```

```python
import functools
import math

import jax
import jax.numpy as jnp
import numpy as np
from jax import lax
from jax.experimental import pallas as pl
from jax.experimental.pallas import tpu as pltpu
from jax.sharding import PartitionSpec as P

FA = 256
FB = 256
HALF = 128
BINS = 16
STEP = 16
BF16 = jnp.bfloat16
F32 = jnp.float32


def waves(rows, cols, length):
    turns = np.outer(rows, cols) % length
    angle = turns * (2.0 * math.pi / length)
    return np.cos(angle), np.sin(angle)


def tables():
    bf = np.dtype(BF16)
    every = np.arange(FA)
    cosine, sine = waves(every, every, FA)
    first = np.block([[cosine, -sine], [sine, cosine]]).astype(bf)
    half = np.arange(HALF)
    even_c, even_s = waves(half, 2 * half, FA)
    odd_c, odd_s = waves(half, 2 * half + 1, FA)
    second = np.stack(
        [
            np.block([[even_c, even_s], [-even_s, even_c]]),
            np.block([[odd_c, odd_s], [-odd_s, odd_c]]),
        ]
    ).astype(bf)
    coarse = np.block([[cosine, sine], [-sine, cosine]]).astype(np.float32)
    upper = coarse.astype(bf)
    lower = (coarse - upper.astype(np.float32)).astype(bf)
    turn = np.stack(waves(every, every, FA * FB)).astype(np.float32)
    return first, second, np.stack([upper, lower]), turn


def dot(left, right):
    return jnp.dot(left, right, preferred_element_type=F32)


def split(value):
    upper = value.astype(BF16)
    return upper, (value - upper.astype(F32)).astype(BF16)


def doublings(nseg):
    flips = [1 << k for k in range(1, nseg.bit_length() - 1)]
    return flips[::-1], flips


def holdings(nseg):
    if nseg == 8:
        return [0, 6, 4, 2], [0, 6, 4, 2]
    held = []
    for order in doublings(nseg):
        flips = [0]
        for flip in order:
            flips = flips + [x ^ flip for x in flips]
        held.append(flips)
    return held


def filter_body(
    nseg, held, flips, live_ref, edges_ref, halves, slots, first_ref, second_ref, turn_ref,
    sums, tops, powers, lefts, spectra, products, firsts, turneds, series,
):
    evens, odds = holdings(nseg)
    my_bank = lax.axis_index("bank")
    my_seg = lax.axis_index("seg")
    core = my_seg & 1
    rows = FB // nseg
    low = nseg // 2
    tiles = powers.shape[0] // len(flips)
    blocks = lax.broadcasted_iota(jnp.int32, (BINS, FB), 1)
    bins = lax.broadcasted_iota(jnp.int32, (BINS, FB), 0)

    def stage(n):
        q, k = n // tiles, n % tiles
        left, spectrum = lefts[n % 2], spectra[n % 2]
        t = owner(my_bank, core, flips[q]) * tiles + k
        (mine, mine_at), (theirs, theirs_at) = halves[q]
        for z in range(low):
            even, odd = evens[z], odds[z]
            own = my_seg ^ jnp.where(core == 0, even, odd)
            other = my_seg ^ 1 ^ jnp.where(core == 0, odd, even)
            for ref, at, seg in ((mine, mine_at, own), (theirs, theirs_at, other)):
                start = pl.multiple_of(seg * rows, rows)
                spectrum[:, pl.ds(start, rows), :] = ref[(at + z) * tiles + k].astype(F32)
        label = jnp.zeros((BINS, FB), jnp.int32)
        for j in range(BINS - 1):
            label = label + (edges_ref[t, j] <= blocks).astype(jnp.int32)
        onehot = (label == bins).astype(F32).astype(BF16)
        nothing = jnp.zeros((BINS, FB), BF16)
        left[0 : 2 * FB] = first_ref[...]
        left[2 * FB : 2 * FB + BINS, 0:FB] = onehot
        left[2 * FB : 2 * FB + BINS, FB:] = nothing
        left[2 * FB + BINS :, 0:FB] = nothing
        left[2 * FB + BINS :, FB:] = onehot
        energy = spectrum[0] * spectrum[0] + spectrum[1] * spectrum[1]
        energy = energy[:, :HALF] + energy[:, HALF:]
        upper, lower = split(energy)
        powers[n] = dot(onehot, upper) + dot(onehot, lower)

    def multiply(u):
        n, s = u // held, u % held
        spectrum = spectra[n % 2]
        for r in range(0, FB, STEP):
            lines = slice(r, r + STEP)
            hre, him = spectrum[0, lines], spectrum[1, lines]
            for d in range(2):
                sre = slots[s][d, 0, lines].astype(F32)
                sim = slots[s][d, 1, lines].astype(F32)
                product = products[u % 2 * 2 + d]
                product[lines] = (sre * hre + sim * him).astype(BF16)
                product[FB + r : FB + r + STEP] = (sim * hre - sre * him).astype(BF16)

    def transform(u, d):
        at = u % 2 * 2 + d
        firsts[at][...] = dot(lefts[u // held % 2][...], products[at][...])

    def turn_round(u, d):
        first, turned = firsts[u % 2 * 2 + d], turneds[u % 2 * 2 + d]
        for r in range(0, FB, STEP):
            out = slice(r, r + STEP)
            are, aim = first[out], first[FB + r : FB + r + STEP]
            cos, sin = turn_ref[0, out], turn_ref[1, out]
            bre = are * cos - aim * sin
            bim = are * sin + aim * cos
            turned[0, out, 0:HALF] = (bre[:, :HALF] + bre[:, HALF:]).astype(BF16)
            turned[0, out, HALF:] = (bim[:, :HALF] + bim[:, HALF:]).astype(BF16)
            turned[1, out, 0:HALF] = (bre[:, :HALF] - bre[:, HALF:]).astype(BF16)
            turned[1, out, HALF:] = (bim[:, :HALF] - bim[:, HALF:]).astype(BF16)
        base = (u * 2 + d) * BINS
        sums[base : base + BINS, 0:FA] = first[2 * FB : 2 * FB + BINS]
        sums[base : base + BINS, FA:] = first[2 * FB + BINS :]

    def finish(u, d):
        at = u % 2 * 2 + d
        for parity in range(2):
            series[at][parity] = dot(turneds[at][parity], second_ref[parity])

    def highest(u):
        best = None
        ones, twos = series[u % 2 * 2], series[u % 2 * 2 + 1]
        for parity in range(2):
            for r in range(0, FB, STEP):
                one, two = ones[parity, r : r + STEP], twos[parity, r : r + STEP]
                both = one * one + two * two
                both = both[:, :HALF] + both[:, HALF:]
                best = both if best is None else jnp.maximum(best, both)
        tops[u] = best

    units = powers.shape[0] * held
    stage(0)
    multiply(0)
    transform(0, 0)
    transform(0, 1)
    for u in range(units):
        more = u + 1 < units
        if more:
            if (u + 1) % held == 0:
                stage((u + 1) // held)
            multiply(u + 1)
        turn_round(u, 0)
        if more:
            transform(u + 1, 0)
        finish(u, 0)
        turn_round(u, 1)
        if more:
            transform(u + 1, 1)
        if u > 0:
            highest(u - 1)
        finish(u, 1)
    highest(units - 1)


def owner(my_bank, core, flip):
    return my_bank ^ (flip[0] if flip[0] == flip[1] else jnp.where(core == 0, flip[0], flip[1]))


def statistics(
    held, flips, live_ref, coarse_ref, groups, before, peak_ref, snr_ref, chi_ref, gathered, parts
):
    my_bank = lax.axis_index("bank")
    core = lax.axis_index("seg") & 1
    tiles = groups[0][2].shape[0]
    at = 0
    for sums, _, _ in groups:
        gathered[at : at + sums.shape[0]] = sums[...]
        at += sums.shape[0]
    upper, lower = split(gathered[...])
    parts[...] = dot(upper, coarse_ref[0]) + dot(lower, coarse_ref[0]) + dot(upper, coarse_ref[1])
    peaks = jnp.zeros(peak_ref.shape, F32)
    if before:
        peaks = before[0][...]
        snr_ref[...] = before[1][...]
        chi_ref[...] = before[2][...]
    slot_at = lax.broadcasted_iota(jnp.int32, peak_ref.shape, 0)
    tile_at = lax.broadcasted_iota(jnp.int32, peak_ref.shape, 1)
    n = 0
    for _, tops, powers in groups:
        for k in range(powers.shape[0]):
            t = owner(my_bank, core, flips[n // tiles]) * tiles + n % tiles
            hpower = jnp.sum(powers[k], axis=1, keepdims=True)
            sigma = jnp.sum(hpower, axis=0, keepdims=True)
            share = hpower / sigma
            for s in range(held):
                live = live_ref[s] != 0
                base = (n * held + s) * 2 * BINS
                snr = jnp.zeros((1, FB), F32)
                chi = jnp.zeros((1, FB), F32)
                for d in range(2):
                    own = parts[base + d * BINS : base + (d + 1) * BINS]
                    whole = jnp.sum(own, axis=0, keepdims=True)
                    diff = own - share * whole
                    diff = jnp.sum(diff * diff, axis=0, keepdims=True)
                    whole = whole * whole
                    snr = snr + whole[:, :FB] + whole[:, FB:]
                    chi = chi + diff[:, :FB] + diff[:, FB:]
                snr_ref[t, s : s + 1] = jnp.where(live, snr / sigma, 0.0)
                chi = chi / sigma / (4.0 * (BINS - 1))
                chi_ref[t, s : s + 1] = jnp.where(live, chi, 0.0)
                top = jnp.max(tops[k * held + s], axis=0, keepdims=True)
                top = jnp.sqrt(jnp.max(top, axis=1, keepdims=True) / sigma)
                peaks = jnp.where((slot_at == s) & (tile_at == t) & live, top, peaks)
            n += 1
    peak_ref[...] = peaks


def on_device(nbank, nseg, strain, templates, bin_edges, live_flags):
    held = strain.shape[0]
    tiles = templates.shape[0]
    total = tiles * nbank
    rows = FB // nseg
    low = nseg // 2
    first, second, coarse, turn = (jnp.asarray(x) for x in tables())
    smem = pl.BlockSpec(memory_space=pltpu.SMEM)
    vmem = pl.BlockSpec(memory_space=pltpu.VMEM)

    def swap(block, flips):
        route = []
        for b in range(nbank):
            for s in range(nseg):
                flip_bank, flip_seg = flips[s & 1]
                route.append((b * nseg + s, (b ^ flip_bank) * nseg + (s ^ flip_seg)))
        return lax.ppermute(block, ("bank", "seg"), route)

    twin = ((0, 1), (0, 1))

    def call(flips, arrays, halves, earlier=None, before=()):
        fresh = len(flips) * tiles
        made = [
            jax.ShapeDtypeStruct((fresh * held * 2 * BINS, 2 * FA), F32),
            jax.ShapeDtypeStruct((fresh * held, STEP, HALF), F32),
            jax.ShapeDtypeStruct((fresh, BINS, HALF), F32),
        ]
        scratch = [
            [pltpu.VMEM((2 * FB + 2 * BINS, 2 * FB), BF16) for _ in range(2)],
            [pltpu.VMEM((2, FB, FA), F32) for _ in range(2)],
            [pltpu.VMEM((2 * FB, FA), BF16) for _ in range(4)],
            [pltpu.VMEM((2 * FB + 2 * BINS, FA), F32) for _ in range(4)],
            [pltpu.VMEM((2, FB, FA), BF16) for _ in range(4)],
            [pltpu.VMEM((2, FB, FA), F32) for _ in range(4)],
        ]
        count = len(arrays)

        def run(live_ref, edges_ref, first_ref, second_ref, turn_ref, *rest):
            slots, rest = rest[:held], rest[held:]
            spectra, rest = rest[:count], rest[count:]
            pairs = [[(spectra[i], at) for i, at in half] for half in halves]
            if earlier is None:
                results, scratches = rest[:3], rest[3:]
            else:
                coarse_ref, rest = rest[0], rest[1:]
                groups = [rest[i : i + 3] for i in range(0, 3 * len(earlier[1]), 3)]
                rest = rest[3 * len(groups) :]
                older, rest = rest[: len(before)], rest[len(before) :]
                outs, results, scratches = rest[:3], rest[3:6], rest[8:]
            filter_body(
                nseg, held, flips, live_ref, edges_ref, pairs, slots,
                first_ref, second_ref, turn_ref, *results, *scratches,
            )
            if earlier is not None:
                every = earlier[0] + flips
                groups = groups + [results]
                statistics(held, every, live_ref, coarse_ref, groups, older, *outs, *rest[6:8])

        inputs = [live_flags, bin_edges, first, second, turn, *slots, *arrays]
        if earlier is None:
            shapes = made
        else:
            inputs += [coarse] + [x for group in earlier[1] for x in group] + list(before)
            shapes = [
                jax.ShapeDtypeStruct((held, total), F32),
                jax.ShapeDtypeStruct((total, held, FB), F32),
                jax.ShapeDtypeStruct((total, held, FB), F32),
            ]
            every = (len(earlier[1]) + 1) * fresh
            full = pltpu.VMEM((every * held * 2 * BINS, 2 * FA), F32)
            scratch = [pltpu.VMEM(x.shape, x.dtype) for x in made] + [full, full] + scratch
        return pl.pallas_call(
            run,
            in_specs=[smem, smem] + [vmem] * (len(inputs) - 2),
            out_specs=[vmem] * 3,
            out_shape=shapes,
            scratch_shapes=scratch,
            compiler_params=pltpu.CompilerParams(vmem_limit_bytes=24 << 20),
            cost_estimate=pl.CostEstimate(
                flops=1 * fresh * held * 2 * 12 * FA**3, bytes_accessed=1 << 20, transcendentals=0
            ),
        )(*inputs)

    block = templates if nseg == 8 else templates.reshape(tiles, 2, rows, FA)
    slots = []

    def slot_beside(found, strain):
        slot = strain[len(slots)].reshape(2, 2, FB, FA)
        found, slot, strain = lax.optimization_barrier((found, slot, strain))
        slots.append(slot)
        return found, strain

    if nseg == 8:
        third, second_, near = (swap(block, ((0, x), (0, x))) for x in (6, 4, 2))
        third, strain = slot_beside(third, strain)
        near, strain = slot_beside(near, strain)
        block = jnp.concatenate([block, third, second_, near], axis=0).reshape(low * tiles, 2, rows, FA)
    else:
        for even, odd in zip(*doublings(nseg)):
            found = swap(block, ((0, even), (0, odd)))
            if len(slots) < held:
                found, strain = slot_beside(found, strain)
            block = jnp.concatenate([block, found], axis=0)
    other = swap(block, twin)
    one = swap(block, ((1, 0), (2, 0)))
    two = swap(block, ((2, 0), (1, 0)))
    while len(slots) < held:
        slots.append(strain[len(slots)].reshape(2, 2, FB, FA))
    here = call([(0, 0)], [block, other], [((0, 0), (1, 0))])
    one, two, here = lax.optimization_barrier((one, two, here))
    others = swap(jnp.concatenate([one, two], axis=0), twin)
    corner = swap(one, ((2, 0), (1, 0)))
    beside = call(
        [(1, 2)], [one, others], [((0, 0), (1, low))], ([(0, 0)], [here])
    )
    corner, beside = lax.optimization_barrier((corner, beside))
    other_corner = swap(corner, twin)
    across = call([(2, 1)], [two, others], [((0, 0), (1, 0))])
    other_corner, across = lax.optimization_barrier((other_corner, across))
    peak, snr, chi = call(
        [(3, 3)],
        [corner, other_corner],
        [((0, 0), (1, 0))],
        ([(2, 1)], [across]),
        beside,
    )
    return peak.T, snr, chi


def solution(mesh):
    in_specs = (
        P(("bank", "seg"), None, None, None),
        P("bank", None, "seg"),
        P(),
        P(("bank", "seg")),
    )
    out_specs = (
        P(None, ("bank", "seg")),
        P(None, ("bank", "seg"), None),
        P(None, ("bank", "seg"), None),
    )
    body = functools.partial(on_device, mesh.shape["bank"], mesh.shape["seg"])
    return jax.shard_map(body, mesh=mesh, in_specs=in_specs, out_specs=out_specs, check_vma=False)
```

```python
import functools
import math

import jax
import jax.numpy as jnp
import numpy as np
from jax import lax
from jax.experimental import pallas as pl
from jax.experimental.pallas import tpu as pltpu
from jax.sharding import PartitionSpec as P

FA = 256
FB = 256
HALF = 128
BINS = 16
STEP = 16
BF16 = jnp.bfloat16
F32 = jnp.float32


def waves(rows, cols, length):
    turns = np.outer(rows, cols) % length
    angle = turns * (2.0 * math.pi / length)
    return np.cos(angle), np.sin(angle)


def tables():
    bf = np.dtype(BF16)
    every = np.arange(FA)
    cosine, sine = waves(every, every, FA)
    half = np.arange(HALF)
    even_c, even_s = waves(half, 2 * half, FA)
    odd_c, odd_s = waves(half, 2 * half + 1, FA)
    second = np.stack(
        [
            np.block([[even_c, even_s], [-even_s, even_c]]),
            np.block([[odd_c, odd_s], [-odd_s, odd_c]]),
        ]
    ).astype(bf)
    coarse = np.block([[cosine, sine], [-sine, cosine]]).astype(np.float32)
    upper = coarse.astype(bf)
    lower = (coarse - upper.astype(np.float32)).astype(bf)
    samples = np.concatenate([2 * half, 2 * half + 1])
    turn = np.stack(waves(samples, every, FA * FB)).astype(np.float32)
    first = np.transpose(second, (0, 2, 1))
    return first, second, np.stack([upper, lower]), turn


def dot(left, right):
    return jnp.dot(left, right, preferred_element_type=F32)


def split(value):
    upper = value.astype(BF16)
    return upper, (value - upper.astype(F32)).astype(BF16)


def bin_table(edges):
    ends = jnp.full((edges.shape[0], 1), FB, edges.dtype)
    low = jnp.concatenate([ends - FB, edges], axis=1)[:, :, None]
    high = jnp.concatenate([edges, ends], axis=1)[:, :, None]
    blocks = jnp.arange(FB, dtype=edges.dtype)[None, None, :]
    return ((low <= blocks) & (blocks < high)).astype(BF16)


def doublings(nseg):
    flips = [1 << k for k in range(1, nseg.bit_length() - 1)]
    return flips[::-1], flips


def holdings(nseg):
    if nseg == 8:
        return [0, 6, 4, 2], [0, 6, 4, 2]
    held = []
    for order in doublings(nseg):
        flips = [0]
        for flip in order:
            flips = flips + [x ^ flip for x in flips]
        held.append(flips)
    return held


def filter_body(
    nseg, held, flips, bins_ref, halves, slots, first_ref, second_ref, turn_ref,
    sums, tops, powers, lefts, spectra, products, firsts, turneds, series,
):
    evens, odds = holdings(nseg)
    my_bank = lax.axis_index("bank")
    my_seg = lax.axis_index("seg")
    core = my_seg & 1
    rows = FB // nseg
    low = nseg // 2
    tiles = powers.shape[0] // len(flips)

    def stage(n):
        q, k = n // tiles, n % tiles
        left, spectrum = lefts[n % 2], spectra[n % 2]
        t = owner(my_bank, core, flips[q]) * tiles + k
        (mine, mine_at), (theirs, theirs_at) = halves[q]
        for z in range(low):
            even, odd = evens[z], odds[z]
            own = my_seg ^ jnp.where(core == 0, even, odd)
            other = my_seg ^ 1 ^ jnp.where(core == 0, odd, even)
            for ref, at, seg in ((mine, mine_at, own), (theirs, theirs_at, other)):
                start = pl.multiple_of(seg * rows, rows)
                spectrum[:, pl.ds(start, rows), :] = ref[(at + z) * tiles + k].astype(F32)
        onehot = bins_ref[t]
        nothing = jnp.zeros((BINS, HALF), BF16)
        lead = onehot.astype(F32)
        lead, trail = 0.5 * lead[:, :HALF], 0.5 * lead[:, HALF:]
        for parity, mean in enumerate((lead + trail, lead - trail)):
            mean = mean.astype(BF16)
            left[parity, 0:FB] = first_ref[parity]
            left[parity, FB : FB + BINS, 0:HALF] = mean
            left[parity, FB : FB + BINS, HALF:] = nothing
            left[parity, FB + BINS :, 0:HALF] = nothing
            left[parity, FB + BINS :, HALF:] = mean
        energy = spectrum[0] * spectrum[0] + spectrum[1] * spectrum[1]
        energy = energy[:, :HALF] + energy[:, HALF:]
        upper, lower = split(energy)
        powers[n] = dot(onehot, upper) + dot(onehot, lower)

    def multiply(u):
        n, s = u // held, u % held
        spectrum = spectra[n % 2]
        for r in range(0, HALF, STEP):
            out = slice(r, r + STEP)
            for d in range(2):
                product, pair = products[u % 2 * 2 + d], []
                for at in (r, r + HALF):
                    lines = slice(at, at + STEP)
                    hre, him = spectrum[0, lines], spectrum[1, lines]
                    sre = slots[s][d, 0, lines].astype(F32)
                    sim = slots[s][d, 1, lines].astype(F32)
                    pair.append((sre * hre + sim * him, sim * hre - sre * him))
                (are, aim), (bre, bim) = pair
                product[0, out] = (are + bre).astype(BF16)
                product[0, HALF + r : HALF + r + STEP] = (aim + bim).astype(BF16)
                product[1, out] = (are - bre).astype(BF16)
                product[1, HALF + r : HALF + r + STEP] = (aim - bim).astype(BF16)

    results = {}

    def transform(u, d):
        at = u % 2 * 2 + d
        for parity in range(2):
            results[u, d, parity] = dot(lefts[u // held % 2][parity], products[at][parity])

    def turn_round(u, d):
        turned = turneds[u % 2 * 2 + d]
        for r in range(0, FB, STEP):
            out, parity, at = slice(r, r + STEP), r // HALF, r % HALF
            first = results[u, d, parity]
            are, aim = first[at : at + STEP], first[HALF + at : HALF + at + STEP]
            cos, sin = turn_ref[0, out], turn_ref[1, out]
            bre = are * cos - aim * sin
            bim = are * sin + aim * cos
            turned[0, out, 0:HALF] = (bre[:, :HALF] + bre[:, HALF:]).astype(BF16)
            turned[0, out, HALF:] = (bim[:, :HALF] + bim[:, HALF:]).astype(BF16)
            turned[1, out, 0:HALF] = (bre[:, :HALF] - bre[:, HALF:]).astype(BF16)
            turned[1, out, HALF:] = (bim[:, :HALF] - bim[:, HALF:]).astype(BF16)
        base = (u * 2 + d) * BINS
        inner = slice(FB, FB + BINS)
        outer = slice(FB + BINS, FB + 2 * BINS)
        sums[base : base + BINS, 0:FA] = results[u, d, 0][inner] + results[u, d, 1][inner]
        sums[base : base + BINS, FA:] = results[u, d, 0][outer] + results[u, d, 1][outer]

    def finish(u, d):
        at = u % 2 * 2 + d
        best = None
        for parity in range(2):
            result = dot(turneds[at][parity], second_ref[parity])
            for r in range(0, FB, STEP):
                one = result[r : r + STEP]
                one = one * one
                one = one[:, :HALF] + one[:, HALF:]
                if d == 0:
                    series[u % 2][parity, r : r + STEP] = one
                else:
                    one = one + series[u % 2][parity, r : r + STEP]
                    best = one if best is None else jnp.maximum(best, one)
        if d == 1:
            tops[u] = best

    units = powers.shape[0] * held
    stage(0)
    multiply(0)
    transform(0, 0)
    transform(0, 1)
    for u in range(units):
        more = u + 1 < units
        if more:
            if (u + 1) % held == 0:
                stage((u + 1) // held)
            multiply(u + 1)
        turn_round(u, 0)
        if more:
            transform(u + 1, 0)
        finish(u, 0)
        turn_round(u, 1)
        if more:
            transform(u + 1, 1)
        finish(u, 1)


def owner(my_bank, core, flip):
    return my_bank ^ (flip[0] if flip[0] == flip[1] else jnp.where(core == 0, flip[0], flip[1]))


def statistics(
    held, flips, live_ref, coarse_ref, groups, before, peak_ref, snr_ref, chi_ref, gathered, parts
):
    my_bank = lax.axis_index("bank")
    core = lax.axis_index("seg") & 1
    tiles = groups[0][2].shape[0]
    at = 0
    for sums, _, _ in groups:
        gathered[at : at + sums.shape[0]] = sums[...]
        at += sums.shape[0]
    upper, lower = split(gathered[...])
    parts[...] = dot(upper, coarse_ref[0]) + dot(lower, coarse_ref[0]) + dot(upper, coarse_ref[1])
    peaks = jnp.zeros(peak_ref.shape, F32)
    if before:
        peaks = before[0][...]
        snr_ref[...] = before[1][...]
        chi_ref[...] = before[2][...]
    slot_at = lax.broadcasted_iota(jnp.int32, peak_ref.shape, 0)
    tile_at = lax.broadcasted_iota(jnp.int32, peak_ref.shape, 1)
    n = 0
    for _, tops, powers in groups:
        for k in range(powers.shape[0]):
            t = owner(my_bank, core, flips[n // tiles]) * tiles + n % tiles
            hpower = jnp.sum(powers[k], axis=1, keepdims=True)
            sigma = jnp.sum(hpower, axis=0, keepdims=True)
            share = hpower / sigma
            for s in range(held):
                live = live_ref[0:1, s : s + 1].astype(F32)
                lives = jnp.broadcast_to(live, (1, FB)) > 0
                base = (n * held + s) * 2 * BINS
                snr = jnp.zeros((1, FB), F32)
                chi = jnp.zeros((1, FB), F32)
                for d in range(2):
                    own = parts[base + d * BINS : base + (d + 1) * BINS]
                    whole = jnp.sum(own, axis=0, keepdims=True)
                    diff = own - share * whole
                    diff = jnp.sum(diff * diff, axis=0, keepdims=True)
                    whole = whole * whole
                    snr = snr + whole[:, :FB] + whole[:, FB:]
                    chi = chi + diff[:, :FB] + diff[:, FB:]
                snr_ref[t, s : s + 1] = jnp.where(lives, snr / sigma, 0.0)
                chi = chi / sigma / (4.0 * (BINS - 1))
                chi_ref[t, s : s + 1] = jnp.where(lives, chi, 0.0)
                top = jnp.max(tops[k * held + s], axis=0, keepdims=True)
                top = jnp.sqrt(jnp.max(top, axis=1, keepdims=True) / sigma)
                top = jnp.where(live > 0, top, 0.0)
                peaks = jnp.where((slot_at == s) & (tile_at == t), top, peaks)
            n += 1
    peak_ref[...] = peaks


def on_device(nbank, nseg, strain, templates, bin_edges, live_flags):
    held = strain.shape[0]
    tiles = templates.shape[0]
    total = tiles * nbank
    rows = FB // nseg
    low = nseg // 2
    first, second, coarse, turn = (jnp.asarray(x) for x in tables())
    vmem = pl.BlockSpec(memory_space=pltpu.VMEM)

    def swap(block, flips):
        route = []
        for b in range(nbank):
            for s in range(nseg):
                flip_bank, flip_seg = flips[s & 1]
                route.append((b * nseg + s, (b ^ flip_bank) * nseg + (s ^ flip_seg)))
        return lax.ppermute(block, ("bank", "seg"), route)

    twin = ((0, 1), (0, 1))

    def call(flips, arrays, halves, earlier=None, before=()):
        fresh = len(flips) * tiles
        made = [
            jax.ShapeDtypeStruct((fresh * held * 2 * BINS, 2 * FA), F32),
            jax.ShapeDtypeStruct((fresh * held, STEP, HALF), F32),
            jax.ShapeDtypeStruct((fresh, BINS, HALF), F32),
        ]
        scratch = [
            [pltpu.VMEM((2, FB + 2 * BINS, FB), BF16) for _ in range(2)],
            [pltpu.VMEM((2, FB, FA), F32) for _ in range(2)],
            [pltpu.VMEM((2, FB, FA), BF16) for _ in range(4)],
            [pltpu.VMEM((2, FB + 2 * BINS, FA), F32) for _ in range(4)],
            [pltpu.VMEM((2, FB, FA), BF16) for _ in range(4)],
            [pltpu.VMEM((2, FB, HALF), F32) for _ in range(2)],
        ]
        count = len(arrays)

        def run(live_ref, bins_ref, first_ref, second_ref, turn_ref, *rest):
            slots, rest = rest[:held], rest[held:]
            spectra, rest = rest[:count], rest[count:]
            pairs = [[(spectra[i], at) for i, at in half] for half in halves]
            if earlier is None:
                results, scratches = rest[:3], rest[3:]
            else:
                coarse_ref, rest = rest[0], rest[1:]
                groups = [rest[i : i + 3] for i in range(0, 3 * len(earlier[1]), 3)]
                rest = rest[3 * len(groups) :]
                older, rest = rest[: len(before)], rest[len(before) :]
                outs, results, scratches = rest[:3], rest[3:6], rest[8:]
            filter_body(
                nseg, held, flips, bins_ref, pairs, slots,
                first_ref, second_ref, turn_ref, *results, *scratches,
            )
            if earlier is not None:
                every = earlier[0] + flips
                groups = groups + [results]
                statistics(held, every, live_ref, coarse_ref, groups, older, *outs, *rest[6:8])

        inputs = [live_flags.reshape(1, held), onehot, first, second, turn, *slots, *arrays]
        if earlier is None:
            shapes = made
        else:
            inputs += [coarse] + [x for group in earlier[1] for x in group] + list(before)
            shapes = [
                jax.ShapeDtypeStruct((held, total), F32),
                jax.ShapeDtypeStruct((total, held, FB), F32),
                jax.ShapeDtypeStruct((total, held, FB), F32),
            ]
            every = (len(earlier[1]) + 1) * fresh
            full = pltpu.VMEM((every * held * 2 * BINS, 2 * FA), F32)
            scratch = [pltpu.VMEM(x.shape, x.dtype) for x in made] + [full, full] + scratch
        return pl.pallas_call(
            run,
            in_specs=[vmem] * len(inputs),
            out_specs=[vmem] * 3,
            out_shape=shapes,
            scratch_shapes=scratch,
            compiler_params=pltpu.CompilerParams(vmem_limit_bytes=24 << 20),
            cost_estimate=pl.CostEstimate(
                flops=1 * fresh * held * 2 * 12 * FA**3, bytes_accessed=1 << 20, transcendentals=0
            ),
        )(*inputs)

    block = templates if nseg == 8 else templates.reshape(tiles, 2, rows, FA)
    slots = []

    def slot_beside(found, strain):
        slot = strain[len(slots)].reshape(2, 2, FB, FA)
        found, slot, strain = lax.optimization_barrier((found, slot, strain))
        slots.append(slot)
        return found, strain

    if nseg == 8:
        third, second_, near = (swap(block, ((0, x), (0, x))) for x in (6, 4, 2))
        third, strain = slot_beside(third, strain)
        third, bin_edges = lax.optimization_barrier((third, bin_edges))
        onehot = bin_table(bin_edges)
        near, onehot = lax.optimization_barrier((near, onehot))
        near, strain = slot_beside(near, strain)
        block = jnp.concatenate([block, third, second_, near], axis=0).reshape(low * tiles, 2, rows, FA)
    else:
        onehot = bin_table(bin_edges)
        for even, odd in zip(*doublings(nseg)):
            found = swap(block, ((0, even), (0, odd)))
            if len(slots) < held:
                found, strain = slot_beside(found, strain)
            block = jnp.concatenate([block, found], axis=0)
    other = swap(block, twin)
    one = swap(block, ((1, 0), (2, 0)))
    two = swap(block, ((2, 0), (1, 0)))
    while len(slots) < held:
        slots.append(strain[len(slots)].reshape(2, 2, FB, FA))
    here = call([(0, 0)], [block, other], [((0, 0), (1, 0))])
    one, two, here = lax.optimization_barrier((one, two, here))
    others = swap(jnp.concatenate([one, two], axis=0), twin)
    corner = swap(one, ((2, 0), (1, 0)))
    beside = call(
        [(1, 2)], [one, others], [((0, 0), (1, low))], ([(0, 0)], [here])
    )
    corner, beside = lax.optimization_barrier((corner, beside))
    other_corner = swap(corner, twin)
    across = call([(2, 1)], [two, others], [((0, 0), (1, 0))])
    other_corner, across = lax.optimization_barrier((other_corner, across))
    peak, snr, chi = call(
        [(3, 3)],
        [corner, other_corner],
        [((0, 0), (1, 0))],
        ([(2, 1)], [across]),
        beside,
    )
    return peak.T, snr, chi


def solution(mesh):
    in_specs = (
        P(("bank", "seg"), None, None, None),
        P("bank", None, "seg"),
        P(),
        P(("bank", "seg")),
    )
    out_specs = (
        P(None, ("bank", "seg")),
        P(None, ("bank", "seg"), None),
        P(None, ("bank", "seg"), None),
    )
    body = functools.partial(on_device, mesh.shape["bank"], mesh.shape["seg"])
    return jax.shard_map(body, mesh=mesh, in_specs=in_specs, out_specs=out_specs, check_vma=False)
```

```python
import functools
import math

import jax
import jax.numpy as jnp
import numpy as np
from jax import lax
from jax.experimental import pallas as pl
from jax.experimental.pallas import tpu as pltpu
from jax.sharding import PartitionSpec as P

FA = 256
FB = 256
HALF = 128
BINS = 16
STEP = 16
BF16 = jnp.bfloat16
F32 = jnp.float32


def waves(rows, cols, length):
    turns = np.outer(rows, cols) % length
    angle = turns * (2.0 * math.pi / length)
    return np.cos(angle), np.sin(angle)


def tables():
    bf = np.dtype(BF16)
    every = np.arange(FA)
    cosine, sine = waves(every, every, FA)
    first = np.block([[cosine, -sine], [sine, cosine]]).astype(bf)
    half = np.arange(HALF)
    even_c, even_s = waves(half, 2 * half, FA)
    odd_c, odd_s = waves(half, 2 * half + 1, FA)
    second = np.stack(
        [
            np.block([[even_c, even_s], [-even_s, even_c]]),
            np.block([[odd_c, odd_s], [-odd_s, odd_c]]),
        ]
    ).astype(bf)
    coarse = np.block([[cosine, sine], [-sine, cosine]]).astype(np.float32)
    upper = coarse.astype(bf)
    lower = (coarse - upper.astype(np.float32)).astype(bf)
    turn = np.stack(waves(every, every, FA * FB)).astype(np.float32)
    return first, second, np.stack([upper, lower]), turn


def dot(left, right):
    return jnp.dot(left, right, preferred_element_type=F32)


def split(value):
    upper = value.astype(BF16)
    return upper, (value - upper.astype(F32)).astype(BF16)


def bin_table(edges):
    ends = jnp.full((edges.shape[0], 1), FB, edges.dtype)
    low = jnp.concatenate([ends - FB, edges], axis=1)[:, :, None]
    high = jnp.concatenate([edges, ends], axis=1)[:, :, None]
    blocks = jnp.arange(FB, dtype=edges.dtype)[None, None, :]
    return ((low <= blocks) & (blocks < high)).astype(BF16)


def doublings(nseg):
    flips = [1 << k for k in range(1, nseg.bit_length() - 1)]
    return flips[::-1], flips


def holdings(nseg):
    if nseg == 8:
        return [0, 6, 4, 2], [0, 6, 4, 2]
    held = []
    for order in doublings(nseg):
        flips = [0]
        for flip in order:
            flips = flips + [x ^ flip for x in flips]
        held.append(flips)
    return held


def filter_body(
    nseg, held, flips, bins_ref, halves, slots, first_ref, second_ref, turn_ref,
    sums, tops, powers, lefts, spectra, products, turneds, series,
):
    evens, odds = holdings(nseg)
    my_bank = lax.axis_index("bank")
    my_seg = lax.axis_index("seg")
    core = my_seg & 1
    rows = FB // nseg
    low = nseg // 2
    tiles = powers.shape[0] // len(flips)

    def stage(n):
        q, k = n // tiles, n % tiles
        left, spectrum = lefts[n % 2], spectra[n % 2]
        t = owner(my_bank, core, flips[q]) * tiles + k
        (mine, mine_at), (theirs, theirs_at) = halves[q]
        for z in range(low):
            even, odd = evens[z], odds[z]
            own = my_seg ^ jnp.where(core == 0, even, odd)
            other = my_seg ^ 1 ^ jnp.where(core == 0, odd, even)
            for ref, at, seg in ((mine, mine_at, own), (theirs, theirs_at, other)):
                start = pl.multiple_of(seg * rows, rows)
                spectrum[:, pl.ds(start, rows), :] = ref[(at + z) * tiles + k].astype(F32)
        onehot = bins_ref[t]
        nothing = jnp.zeros((BINS, FB), BF16)
        left[0 : 2 * FB] = first_ref[...]
        left[2 * FB : 2 * FB + BINS, 0:FB] = onehot
        left[2 * FB : 2 * FB + BINS, FB:] = nothing
        left[2 * FB + BINS :, 0:FB] = nothing
        left[2 * FB + BINS :, FB:] = onehot
        energy = spectrum[0] * spectrum[0] + spectrum[1] * spectrum[1]
        energy = energy[:, :HALF] + energy[:, HALF:]
        upper, lower = split(energy)
        powers[n] = dot(onehot, upper) + dot(onehot, lower)

    def multiply(u):
        n, s = u // held, u % held
        spectrum = spectra[n % 2]
        for r in range(0, FB, STEP):
            lines = slice(r, r + STEP)
            hre, him = spectrum[0, lines], spectrum[1, lines]
            for d in range(2):
                sre = slots[s][d, 0, lines].astype(F32)
                sim = slots[s][d, 1, lines].astype(F32)
                product = products[u % 2 * 2 + d]
                product[lines] = (sre * hre + sim * him).astype(BF16)
                product[FB + r : FB + r + STEP] = (sim * hre - sre * him).astype(BF16)

    results = {}

    def transform(u, d):
        results[u, d] = dot(lefts[u // held % 2][...], products[u % 2 * 2 + d][...])

    def turn_round(u, d):
        first, turned = results[u, d], turneds[u % 2 * 2 + d]
        for r in range(0, FB, STEP):
            out = slice(r, r + STEP)
            are, aim = first[out], first[FB + r : FB + r + STEP]
            cos, sin = turn_ref[0, out], turn_ref[1, out]
            bre = are * cos - aim * sin
            bim = are * sin + aim * cos
            turned[0, out, 0:HALF] = (bre[:, :HALF] + bre[:, HALF:]).astype(BF16)
            turned[0, out, HALF:] = (bim[:, :HALF] + bim[:, HALF:]).astype(BF16)
            turned[1, out, 0:HALF] = (bre[:, :HALF] - bre[:, HALF:]).astype(BF16)
            turned[1, out, HALF:] = (bim[:, :HALF] - bim[:, HALF:]).astype(BF16)
        base = (u * 2 + d) * BINS
        sums[base : base + BINS, 0:FA] = first[2 * FB : 2 * FB + BINS]
        sums[base : base + BINS, FA:] = first[2 * FB + BINS :]

    def finish(u, d):
        at = u % 2 * 2 + d
        best = None
        for parity in range(2):
            result = dot(turneds[at][parity], second_ref[parity])
            for r in range(0, FB, STEP):
                one = result[r : r + STEP]
                one = one * one
                one = one[:, :HALF] + one[:, HALF:]
                if d == 0:
                    series[u % 2][parity, r : r + STEP] = one
                else:
                    one = one + series[u % 2][parity, r : r + STEP]
                    best = one if best is None else jnp.maximum(best, one)
        if d == 1:
            tops[u] = best

    units = powers.shape[0] * held
    stage(0)
    multiply(0)
    transform(0, 0)
    transform(0, 1)
    for u in range(units):
        more = u + 1 < units
        if more:
            if (u + 1) % held == 0:
                stage((u + 1) // held)
            multiply(u + 1)
        turn_round(u, 0)
        if more:
            transform(u + 1, 0)
        finish(u, 0)
        turn_round(u, 1)
        if more:
            transform(u + 1, 1)
        finish(u, 1)


def owner(my_bank, core, flip):
    return my_bank ^ (flip[0] if flip[0] == flip[1] else jnp.where(core == 0, flip[0], flip[1]))


def statistics(
    held, flips, live_ref, coarse_ref, groups, before, peak_ref, snr_ref, chi_ref, gathered, parts
):
    my_bank = lax.axis_index("bank")
    core = lax.axis_index("seg") & 1
    tiles = groups[0][2].shape[0]
    at = 0
    for sums, _, _ in groups:
        gathered[at : at + sums.shape[0]] = sums[...]
        at += sums.shape[0]
    upper, lower = split(gathered[...])
    parts[...] = dot(upper, coarse_ref[0]) + dot(lower, coarse_ref[0]) + dot(upper, coarse_ref[1])
    peaks = jnp.zeros(peak_ref.shape, F32)
    if before:
        peaks = before[0][...]
        snr_ref[...] = before[1][...]
        chi_ref[...] = before[2][...]
    slot_at = lax.broadcasted_iota(jnp.int32, peak_ref.shape, 0)
    tile_at = lax.broadcasted_iota(jnp.int32, peak_ref.shape, 1)
    n = 0
    for _, tops, powers in groups:
        for k in range(powers.shape[0]):
            t = owner(my_bank, core, flips[n // tiles]) * tiles + n % tiles
            hpower = jnp.sum(powers[k], axis=1, keepdims=True)
            sigma = jnp.sum(hpower, axis=0, keepdims=True)
            share = hpower / sigma
            for s in range(held):
                live = live_ref[0:1, s : s + 1].astype(F32)
                lives = jnp.broadcast_to(live, (1, FB)) > 0
                base = (n * held + s) * 2 * BINS
                snr = jnp.zeros((1, FB), F32)
                chi = jnp.zeros((1, FB), F32)
                for d in range(2):
                    own = parts[base + d * BINS : base + (d + 1) * BINS]
                    whole = jnp.sum(own, axis=0, keepdims=True)
                    diff = own - share * whole
                    diff = jnp.sum(diff * diff, axis=0, keepdims=True)
                    whole = whole * whole
                    snr = snr + whole[:, :FB] + whole[:, FB:]
                    chi = chi + diff[:, :FB] + diff[:, FB:]
                snr_ref[t, s : s + 1] = jnp.where(lives, snr / sigma, 0.0)
                chi = chi / sigma / (4.0 * (BINS - 1))
                chi_ref[t, s : s + 1] = jnp.where(lives, chi, 0.0)
                top = jnp.max(tops[k * held + s], axis=0, keepdims=True)
                top = jnp.sqrt(jnp.max(top, axis=1, keepdims=True) / sigma)
                top = jnp.where(live > 0, top, 0.0)
                peaks = jnp.where((slot_at == s) & (tile_at == t), top, peaks)
            n += 1
    peak_ref[...] = peaks


def on_device(nbank, nseg, strain, templates, bin_edges, live_flags):
    held = strain.shape[0]
    tiles = templates.shape[0]
    total = tiles * nbank
    rows = FB // nseg
    low = nseg // 2
    first, second, coarse, turn = (jnp.asarray(x) for x in tables())
    vmem = pl.BlockSpec(memory_space=pltpu.VMEM)

    def swap(block, flips):
        route = []
        for b in range(nbank):
            for s in range(nseg):
                flip_bank, flip_seg = flips[s & 1]
                route.append((b * nseg + s, (b ^ flip_bank) * nseg + (s ^ flip_seg)))
        return lax.ppermute(block, ("bank", "seg"), route)

    twin = ((0, 1), (0, 1))

    def call(flips, arrays, halves, earlier=None, before=()):
        fresh = len(flips) * tiles
        made = [
            jax.ShapeDtypeStruct((fresh * held * 2 * BINS, 2 * FA), F32),
            jax.ShapeDtypeStruct((fresh * held, STEP, HALF), F32),
            jax.ShapeDtypeStruct((fresh, BINS, HALF), F32),
        ]
        scratch = [
            [pltpu.VMEM((2 * FB + 2 * BINS, 2 * FB), BF16) for _ in range(2)],
            [pltpu.VMEM((2, FB, FA), F32) for _ in range(2)],
            [pltpu.VMEM((2 * FB, FA), BF16) for _ in range(4)],
            [pltpu.VMEM((2, FB, FA), BF16) for _ in range(4)],
            [pltpu.VMEM((2, FB, HALF), F32) for _ in range(2)],
        ]
        count = len(arrays)

        def run(live_ref, bins_ref, first_ref, second_ref, turn_ref, *rest):
            slots, rest = rest[:held], rest[held:]
            spectra, rest = rest[:count], rest[count:]
            pairs = [[(spectra[i], at) for i, at in half] for half in halves]
            if earlier is None:
                results, scratches = rest[:3], rest[3:]
            else:
                coarse_ref, rest = rest[0], rest[1:]
                groups = [rest[i : i + 3] for i in range(0, 3 * len(earlier[1]), 3)]
                rest = rest[3 * len(groups) :]
                older, rest = rest[: len(before)], rest[len(before) :]
                outs, results, scratches = rest[:3], rest[3:6], rest[8:]
            filter_body(
                nseg, held, flips, bins_ref, pairs, slots,
                first_ref, second_ref, turn_ref, *results, *scratches,
            )
            if earlier is not None:
                every = earlier[0] + flips
                groups = groups + [results]
                statistics(held, every, live_ref, coarse_ref, groups, older, *outs, *rest[6:8])

        inputs = [live_flags.reshape(1, held), onehot, first, second, turn, *slots, *arrays]
        if earlier is None:
            shapes = made
        else:
            inputs += [coarse] + [x for group in earlier[1] for x in group] + list(before)
            shapes = [
                jax.ShapeDtypeStruct((held, total), F32),
                jax.ShapeDtypeStruct((total, held, FB), F32),
                jax.ShapeDtypeStruct((total, held, FB), F32),
            ]
            every = (len(earlier[1]) + 1) * fresh
            full = pltpu.VMEM((every * held * 2 * BINS, 2 * FA), F32)
            scratch = [pltpu.VMEM(x.shape, x.dtype) for x in made] + [full, full] + scratch
        return pl.pallas_call(
            run,
            in_specs=[vmem] * len(inputs),
            out_specs=[vmem] * 3,
            out_shape=shapes,
            scratch_shapes=scratch,
            compiler_params=pltpu.CompilerParams(vmem_limit_bytes=24 << 20),
            cost_estimate=pl.CostEstimate(
                flops=1 * fresh * held * 2 * 12 * FA**3, bytes_accessed=1 << 20, transcendentals=0
            ),
        )(*inputs)

    block = templates if nseg == 8 else templates.reshape(tiles, 2, rows, FA)
    slots = []

    def slot_beside(found, strain):
        slot = strain[len(slots)].reshape(2, 2, FB, FA)
        found, slot, strain = lax.optimization_barrier((found, slot, strain))
        slots.append(slot)
        return found, strain

    if nseg == 8:
        third, second_, near = (swap(block, ((0, x), (0, x))) for x in (6, 4, 2))
        third, strain = slot_beside(third, strain)
        third, bin_edges = lax.optimization_barrier((third, bin_edges))
        onehot = bin_table(bin_edges)
        near, onehot = lax.optimization_barrier((near, onehot))
        near, strain = slot_beside(near, strain)
        block = jnp.concatenate([block, third, second_, near], axis=0).reshape(low * tiles, 2, rows, FA)
    else:
        onehot = bin_table(bin_edges)
        for even, odd in zip(*doublings(nseg)):
            found = swap(block, ((0, even), (0, odd)))
            if len(slots) < held:
                found, strain = slot_beside(found, strain)
            block = jnp.concatenate([block, found], axis=0)
    other = swap(block, twin)
    one = swap(block, ((1, 0), (2, 0)))
    two = swap(block, ((2, 0), (1, 0)))
    while len(slots) < held:
        slots.append(strain[len(slots)].reshape(2, 2, FB, FA))
    here = call([(0, 0)], [block, other], [((0, 0), (1, 0))])
    one, two, here = lax.optimization_barrier((one, two, here))
    others = swap(jnp.concatenate([one, two], axis=0), twin)
    corner = swap(one, ((2, 0), (1, 0)))
    beside = call(
        [(1, 2)], [one, others], [((0, 0), (1, low))], ([(0, 0)], [here])
    )
    corner, beside = lax.optimization_barrier((corner, beside))
    other_corner = swap(corner, twin)
    across = call([(2, 1)], [two, others], [((0, 0), (1, 0))])
    other_corner, across = lax.optimization_barrier((other_corner, across))
    peak, snr, chi = call(
        [(3, 3)],
        [corner, other_corner],
        [((0, 0), (1, 0))],
        ([(2, 1)], [across]),
        beside,
    )
    return peak.T, snr, chi


def solution(mesh):
    in_specs = (
        P(("bank", "seg"), None, None, None),
        P("bank", None, "seg"),
        P(),
        P(("bank", "seg")),
    )
    out_specs = (
        P(None, ("bank", "seg")),
        P(None, ("bank", "seg"), None),
        P(None, ("bank", "seg"), None),
    )
    body = functools.partial(on_device, mesh.shape["bank"], mesh.shape["seg"])
    return jax.shard_map(body, mesh=mesh, in_specs=in_specs, out_specs=out_specs, check_vma=False)
```
